256 devices in a mesh: ctx: 64 (over x, z, core), head: 4 (over y).
Axes of the slice: x: 4, y: 4, z: 8, core: 2. Of those that a mesh axis runs over, the one named last changes fastest.
Arguments:
- query: bfloat16 [4096, 64, 192], P('ctx', 'head'), may hold values from -110 to 110
- w_uk: bfloat16 [64, 128, 512], P('head'), may hold values from -0.5 to 0.5
- w_uv: bfloat16 [64, 512, 128], P('head'), may hold values from -0.25 to 0.25
- index_query: bfloat16 [4096, 64, 128], P('ctx', 'head'), may hold values from -1.25 to 1.25
- index_weight: float32 [4096, 64], P('ctx', 'head'), may hold values from -2 to 2
- cache_rows: bfloat16 [131072, 704], P('ctx'), may hold values from -16 to 16
- key_scale: float32 [131072], P('ctx'), may hold values from 0.25 to 4
- selected: int32 [4096, 32], P('ctx'), may hold values from 0 to 2047, as said below
- block_home: int32 [2048], replicated, may hold values from 0 to 2047, as said below
Outputs:
- attn_out: bfloat16 [4096, 64, 128], P('ctx', 'head')
- index_scores: float32 [4096, 2048], P('ctx', 'head')
The draws below stay inside these ranges and needn't reach their ends.
Inputs may be any that keep to these rules, and one draw needn't show every extreme that they name: `selected`: each query names 32 distinct blocks. The queries of one ctx device together name exactly 64 distinct blocks, at most 2 of which sit in the shard of any one ctx device; in every draw one ctx device's shard holds 2 of the blocks of every device. `block_home`: A permutation of the physical blocks.
All inputs are finite; a program needn't handle non-finite values.
Results may differ from the reference program's by a relative error of at most 0.015.
Values may be sent and summed in bfloat16 or wider, within the bound.
A program may use at most 128 MiB of HBM per device.

```python
import math
import jax
import jax.numpy as jnp
from jax import lax

LATENT = 512
ROPE = 64
HEAD_DIM = 128
IHEADS = 64
IDX_DIM = 128
BLOCK = 64
NSEL = 32
HEADS = 64
POOL = 64
BLK_DEV = 32
Q_DEV = 64
CAP = 2
NBLK = 2048
CTX = 131072
Q = 4096
CACHE_W = 704


def block_layout(key):
    base_key = jax.random.fold_in(key, 101)
    home_key, hot_key, pool_key, pick_key = jax.random.split(base_key, 4)
    owners_count = NBLK // BLK_DEV
    homes = jax.random.permutation(home_key, NBLK).astype(jnp.int32)
    hottest = jax.random.randint(hot_key, (), 0, owners_count).astype(jnp.int32)

    def device_pool(dev_key):
        unit_key, slot_key = jax.random.split(dev_key)
        others = jax.random.permutation(unit_key, (owners_count - 1) * CAP)[:POOL - CAP].astype(jnp.int32)
        other_owner = others // CAP
        other_owner = other_owner + (other_owner >= hottest).astype(jnp.int32)
        owners = jnp.concatenate([jnp.zeros((CAP,), jnp.int32) + hottest, other_owner])
        ranks = jnp.concatenate([jnp.arange(CAP, dtype=jnp.int32), others % CAP])
        slot_keys = jax.random.split(slot_key, owners_count)
        slot_table = jax.vmap(lambda one_key: jax.random.permutation(one_key, BLK_DEV)[:CAP])(slot_keys).astype(jnp.int32)
        return owners * BLK_DEV + slot_table[owners, ranks]
    pools = jax.vmap(device_pool)(jax.random.split(pool_key, owners_count))
    inverse = jnp.zeros((NBLK,), jnp.int32).at[homes].set(jnp.arange(NBLK, dtype=jnp.int32))
    logical = inverse[pools]
    half = NSEL // 2

    def query_picks(query_key, position):
        rest = half + jax.random.permutation(query_key, POOL - half)[:half].astype(jnp.int32)
        offsets = jnp.concatenate([jnp.arange(half, dtype=jnp.int32), rest])
        return (position * half + offsets) % POOL
    positions = jnp.arange(Q, dtype=jnp.int32) % Q_DEV
    picks = jax.vmap(query_picks)(jax.random.split(pick_key, Q), positions)
    device = jnp.arange(Q, dtype=jnp.int32) // Q_DEV
    return (homes, logical[device[:, None], picks])


def draw_selected(key, part):
    return block_layout(key)[1]


def draw_block_home(key, part):
    return block_layout(key)[0]


def draw_cache_rows(key, part):
    key = jax.random.fold_in(key, 3)
    noise_key = jax.random.fold_in(key, 0)
    rows = jax.random.normal(noise_key, (CTX, CACHE_W), jnp.float32)
    return jnp.clip(rows, -16.0, 16.0).astype(jnp.bfloat16)


def draw_query(key, part):
    key = jax.random.fold_in(key, 5)
    noise_key = jax.random.fold_in(key, 0)
    rows = jax.random.normal(noise_key, (Q, HEADS, HEAD_DIM + ROPE), jnp.float32)
    return jnp.clip(rows, -110.0, 110.0).astype(jnp.bfloat16)


def block_levels(own_key, shape, cuts, least, largest):
    level = 1.0
    for dim, blocks in cuts:
        steps = jax.random.uniform(jax.random.fold_in(jax.random.fold_in(own_key, 6), dim), (blocks,), jnp.float32, least / len(cuts), largest / len(cuts))
        level = level * jnp.repeat(jnp.exp(steps), shape[dim] // blocks).reshape((-1,) + (1,) * (len(shape) - 1 - dim))
    return level


def centred(key, extent, scale, most, shards=(), kind=jnp.bfloat16):
    entries = jax.random.normal(key, extent, jnp.float32) * scale
    if len(shards) > 0:
        entries = block_levels(key, extent, shards, -0.22, 0.18) * entries
    return jnp.clip(entries, min=-most, max=most).astype(kind)


def setup_inputs(seed: int = 0) -> dict:
    key_of = jax.random.split(jax.random.key(seed), 10)
    query = draw_query(jax.random.fold_in(key_of[9], 71), 0)
    w_uk = centred(key_of[1], (HEADS, HEAD_DIM, LATENT), HEAD_DIM ** -0.5, 0.5, ((0, 4),))
    w_uv = centred(key_of[2], (HEADS, LATENT, HEAD_DIM), LATENT ** -0.5, 0.25, ((0, 4),))
    index_query = centred(key_of[3], (Q, IHEADS, IDX_DIM), (IDX_DIM ** -0.5), 1.25, ((0, 64), (1, 4)))
    index_weight = centred(key_of[4], (Q, IHEADS), (IHEADS ** -0.5), 2.0, ((0, 64), (1, 4)), jnp.float32)
    cache_rows = draw_cache_rows(jax.random.fold_in(key_of[9], 71), 0)
    key_scale = jnp.clip(jnp.exp(math.log(4.0) - 2.7725887 * jax.random.uniform(key_of[6], (CTX,), jnp.float32) ** block_levels(key_of[6], (CTX,), ((0, 64),), -0.2, 0.2)), 0.25, 4.0)
    selected = draw_selected(jax.random.fold_in(key_of[9], 71), 0)
    block_home = draw_block_home(jax.random.fold_in(key_of[9], 71), 0)
    return {"query": query, "w_uk": w_uk, "w_uv": w_uv, "index_query": index_query, "index_weight": index_weight, "cache_rows": cache_rows, "key_scale": key_scale, "selected": selected, "block_home": block_home}


query_group = 16


def reference(query, w_uk, w_uv, index_query, index_weight, cache_rows, key_scale, selected, block_home):
    width = cache_rows.shape[1]
    score_scale = query.shape[-1] ** -0.5
    q_nope = query[..., :HEAD_DIM].astype(jnp.float32)
    q_rope = query[..., HEAD_DIM:]
    q_lat = jnp.einsum("thd,hdc->thc", q_nope, w_uk.astype(jnp.float32)).astype(jnp.bfloat16)
    blocks = cache_rows.reshape(NBLK, BLOCK, width)
    key_scales = key_scale.reshape(NBLK, BLOCK)
    physical = block_home[selected].astype(jnp.int32)
    groups = Q // query_group

    def attend_group(group_args):
        lat_q, rope_q, idx_q, idx_w, where_blocks = group_args
        key_rows = blocks[where_blocks].reshape(query_group, NSEL * BLOCK, width).astype(jnp.float32)
        row_scale = key_scales[where_blocks].reshape(query_group, NSEL * BLOCK)
        latent = key_rows[..., :LATENT]
        rope_part = key_rows[..., LATENT:LATENT + ROPE]
        index_keys = key_rows[..., LATENT + ROPE:]
        scores = jnp.einsum("thc,tsc->ths", lat_q.astype(jnp.float32), latent)
        scores = (scores + jnp.einsum("thr,tsr->ths", rope_q.astype(jnp.float32), rope_part)) * score_scale
        top = jnp.max(scores, axis=-1, keepdims=True)
        expo = jnp.exp(scores - top)
        probs = (expo / jnp.sum(expo, axis=-1, keepdims=True)).astype(jnp.bfloat16)
        context = jnp.einsum("ths,tsc->thc", probs.astype(jnp.float32), latent).astype(jnp.bfloat16)
        raw = jnp.einsum("tjd,tsd->tjs", idx_q.astype(jnp.float32), index_keys)
        weighted = jnp.sum(idx_w[:, :, None] * jnp.maximum(raw, 0.0), axis=1) * row_scale
        return context, weighted

    context, index_scores = lax.map(attend_group, (
        q_lat.reshape(groups, query_group, HEADS, LATENT),
        q_rope.reshape(groups, query_group, HEADS, ROPE),
        index_query.reshape(groups, query_group, IHEADS, IDX_DIM),
        index_weight.reshape(groups, query_group, IHEADS),
        physical.reshape(groups, query_group, NSEL)))
    context = context.reshape(Q, HEADS, LATENT)
    attn_out = jnp.einsum("thc,hcd->thd", context.astype(jnp.float32), w_uv.astype(jnp.float32)).astype(jnp.bfloat16)
    return attn_out, index_scores.reshape(Q, NSEL * BLOCK)
```

```python
import jax
import jax.numpy as jnp
from jax import lax
from jax.experimental import pallas as pl
from jax.experimental.pallas import tpu as pltpu
from jax.sharding import PartitionSpec as P

LATENT = 512
ROPE = 64
HEAD_DIM = 128
IDX_DIM = 128
BLOCK = 64
NSEL = 32
POOL = 64
BLK_DEV = 32
NBLK = 2048
Q_DEV = 64
HEADS_DEV = 16
CTX_DEVS = 64
HEAD_DEVS = 4
PART = BLOCK // HEAD_DEVS
ROWS = HEADS_DEV * Q_DEV
PART_KEYS = POOL * PART
HALF = PART_KEYS // 2
PAIR = 2 * LATENT + 2 * IDX_DIM + 2 * ROPE
NEG = -1e30
MESH = pl.DeviceIdType.MESH
BF = jnp.bfloat16
F32 = jnp.float32


def nn(a, b):
    return jnp.dot(a, b, preferred_element_type=F32)


def nt(a, b):
    return lax.dot_general(a, b, (((1,), (1,)), ((), ())), preferred_element_type=F32)


def iota(shape, dim):
    return lax.broadcasted_iota(jnp.int32, shape, dim)


def onehot(cond):
    return jnp.where(cond, 1.0, 0.0).astype(BF)


def kernel(
    sel_ref,
    home_ref,
    scale_ref,
    iw_ref,
    query_hbm,
    iq_hbm,
    cache_hbm,
    wuk_hbm,
    wuv_hbm,
    attn_ref,
    idx_ref,
    cache_v,
    query_v,
    iq_v,
    wuk_v,
    wuv_v,
    want,
    want_in,
    weights,
    expand,
    served,
    recv,
    posn,
    bias,
    pack0,
    pack1,
    ukeys,
    kv,
    rp,
    iq_all,
    iw_all,
    qlat,
    qra,
    qrb,
    wsum,
    picked,
    picked_in,
    top,
    total,
    acc,
    local_sem,
    req_send,
    req_recv,
    blk_send,
    blk_recv,
    iq_send,
    iq_recv,
    iw_send,
    iw_recv,
    pk_send,
    pk_recv,
    ag_send,
    ag_recv,
    fw_send,
    fw_recv,
):
    me = lax.axis_index("ctx")
    y = lax.axis_index("head")

    def ctx_peer(c):
        return (lax.rem(c + 2 * CTX_DEVS, CTX_DEVS), y)

    def head_peer(d):
        return (me, lax.rem(y + d, HEAD_DEVS))

    barrier = pltpu.get_barrier_semaphore()

    @pl.loop(1, CTX_DEVS)
    def _(s):
        pl.semaphore_signal(barrier, inc=1, device_id=ctx_peer(me + s), device_id_type=MESH)

    for d in range(1, HEAD_DEVS):
        pl.semaphore_signal(barrier, inc=1, device_id=head_peer(d), device_id_type=MESH)

    rows16 = pl.ds(pl.multiple_of(y * PART, PART), PART)
    cp_cache = pltpu.make_async_copy(cache_hbm.at[:, rows16, :], cache_v, local_sem.at[0])
    cp_query = pltpu.make_async_copy(query_hbm, query_v, local_sem.at[1])
    cp_iq = pltpu.make_async_copy(iq_hbm, iq_v, local_sem.at[2])
    cp_wuk = pltpu.make_async_copy(wuk_hbm, wuk_v, local_sem.at[3])
    cp_wuv = pltpu.make_async_copy(wuv_hbm, wuv_v, local_sem.at[4])
    for cp in (cp_cache, cp_query, cp_iq, cp_wuk, cp_wuv):
        cp.start()

    sel = sel_ref[...]
    home = home_ref[...]
    sel_hi = onehot(iota((32, NBLK), 0) == (sel >> 6))
    sel_lo = onehot(iota((64, NBLK), 0) == (sel & 63))
    lane = iota((1, NBLK), 1)
    log_hi = onehot(iota((32, NBLK), 0) == (lane >> 6))
    log_lo = onehot(iota((64, NBLK), 0) == (lane & 63))
    counts = nt(sel_hi, sel_lo)
    wanted = onehot(counts > 0.5)
    wanted_row = jnp.sum(nn(wanted, log_lo) * log_hi.astype(F32), axis=0, keepdims=True)
    rel = (me - (home >> 5)) & (CTX_DEVS - 1)
    holder = jnp.where(iota((CTX_DEVS, NBLK), 0) == rel, 1.0, 0.0)
    slot = onehot(iota((128, NBLK), 0) == (home & (BLK_DEV - 1)))
    want_rel = nt((holder * wanted_row).astype(BF), slot)
    want[...] = want_rel.reshape(CTX_DEVS, 1, 128)
    want_in[0] = want[0]

    pl.semaphore_wait(barrier, CTX_DEVS - 1 + HEAD_DEVS - 1)

    def request(s):
        return pltpu.make_async_remote_copy(
            src_ref=want.at[s],
            dst_ref=want_in.at[s],
            send_sem=req_send.at[s],
            recv_sem=req_recv.at[s],
            device_id=ctx_peer(me - s),
            device_id_type=MESH,
        )

    @pl.loop(1, CTX_DEVS)
    def _(s):
        request(s).start()

    cp_cache.wait()
    rows = cache_v[...].reshape(BLK_DEV * PART, LATENT + ROPE + IDX_DIM)
    pick_scale = iota((BLK_DEV, PART, BLOCK), 2) == y * PART + iota((BLK_DEV, PART, BLOCK), 1)
    scale3 = jnp.broadcast_to(scale_ref[...][:, None, :], (BLK_DEV, PART, BLOCK))
    scale_col = jnp.sum(jnp.where(pick_scale, scale3, 0.0), axis=2, keepdims=True)
    scale_col = scale_col.reshape(BLK_DEV * PART, 1)
    tail = rows[:, LATENT:].astype(F32)
    tail_lane = iota(tail.shape, 1)
    tail = (tail * jnp.where(tail_lane >= ROPE, scale_col, 1.0)).astype(BF)
    src = iota((ROPE + IDX_DIM, 384), 0)
    dst = iota((ROPE + IDX_DIM, 384), 1)
    arrange = onehot(
        ((dst < 128) & (src == dst + ROPE))
        | ((dst >= 128) & (dst < 192) & (src == dst - 128))
        | ((dst >= 320) & (src == dst - 320))
    )
    weights[:, :LATENT] = rows[:, :LATENT]
    weights[:, LATENT:] = nn(tail, arrange).astype(BF)

    @pl.loop(1, CTX_DEVS)
    def _(s):
        request(s).wait_recv()

    asked = want_in[...].reshape(CTX_DEVS, 128)
    before = onehot(iota((128, 128), 0) < iota((128, 128), 1))
    order = nn(asked.astype(BF), before)
    spread = onehot(iota((128, 512), 0) == (iota((128, 512), 1) >> 4))
    for k in range(2):
        first = jnp.where(jnp.abs(order - float(k)) < 0.5, asked, 0.0)
        expand[k] = nn(first.astype(BF), spread)

    def block_copy(s):
        return pltpu.make_async_remote_copy(
            src_ref=served.at[s],
            dst_ref=recv.at[s],
            send_sem=blk_send.at[s],
            recv_sem=blk_recv.at[s],
            device_id=ctx_peer(me + s),
            device_id_type=MESH,
        )

    group = 16

    @pl.loop(0, CTX_DEVS // group)
    def _(i):
        at = pl.ds(pl.multiple_of(i * group, group), group)
        same_row = iota((1, PART, 512), 1) == (iota((1, PART, 512), 2) & (PART - 1))
        gather = []
        for k in range(2):
            wide = jnp.where(same_row, expand[k, at, :][:, None, :], 0.0)
            gather.append(wide.reshape(group * PART, 512).astype(BF))
        o0 = nn(gather[0], weights[:, : LATENT + 256]).astype(BF)
        o1 = nn(gather[1], weights[:, : LATENT + IDX_DIM]).astype(BF)
        r1 = nn(gather[1], weights[:, LATENT + 256 :]).astype(BF)
        shape = (group, PART, -1)
        served[at, :, 0:512] = o0[:, :512].reshape(shape)
        served[at, :, 512:1024] = o1[:, :512].reshape(shape)
        served[at, :, 1024:1152] = o0[:, 512:640].reshape(shape)
        served[at, :, 1152:1280] = o1[:, 512:640].reshape(shape)
        served[at, :, 1280:1408] = (o0[:, 640:768] + r1).reshape(shape)

        @pl.loop(jnp.where(i == 0, 1, 0), group)
        def _(j):
            block_copy(i * group + j).start()

    recv[0] = served[0]

    cp_query.wait()
    cp_iq.wait()
    cp_wuk.wait()
    col = iota((HEAD_DIM + ROPE, 384), 0)
    out = iota((HEAD_DIM + ROPE, 384), 1)
    q_arrange = onehot(
        ((out < 192) & (col == out)) | ((out >= 320) & (col == out - 320 + HEAD_DIM))
    )

    @pl.loop(0, HEADS_DEV)
    def _(h):
        rows_h = pl.ds(pl.multiple_of(h * Q_DEV, Q_DEV), Q_DEV)
        take = onehot(
            iota((Q_DEV, ROWS), 1) == iota((Q_DEV, ROWS), 0) * HEADS_DEV + h
        )
        iq_all[y, rows_h, :] = nn(take, iq_v[...].reshape(ROWS, IDX_DIM)).astype(BF)

    iw_all[y] = iw_ref[...]

    def iq_copy(d):
        return pltpu.make_async_remote_copy(
            src_ref=iq_all.at[y],
            dst_ref=iq_all.at[y],
            send_sem=iq_send.at[d - 1],
            recv_sem=iq_recv.at[d - 1],
            device_id=head_peer(d),
            device_id_type=MESH,
        )

    def iw_copy(d):
        return pltpu.make_async_remote_copy(
            src_ref=iw_all.at[y],
            dst_ref=iw_all.at[y],
            send_sem=iw_send.at[d - 1],
            recv_sem=iw_recv.at[d - 1],
            device_id=head_peer(d),
            device_id_type=MESH,
        )

    for d in range(1, HEAD_DEVS):
        iq_copy(d).start()
        iw_copy(d).start()

    @pl.loop(0, HEADS_DEV)
    def _(h):
        rows_h = pl.ds(pl.multiple_of(h * Q_DEV, Q_DEV), Q_DEV)
        take = onehot(
            iota((Q_DEV, ROWS), 1) == iota((Q_DEV, ROWS), 0) * HEADS_DEV + h
        )
        mine = nn(take, query_v[...].reshape(ROWS, HEAD_DIM + ROPE)).astype(BF)
        parts = nn(mine, q_arrange).astype(BF)
        qlat[rows_h, :] = nn(parts[:, :HEAD_DIM], wuk_v[h]).astype(BF)
        qra[rows_h, :] = parts[:, 128:256]
        qrb[rows_h, :] = parts[:, 256:384]

    asked_rel = want[...].reshape(CTX_DEVS, 128).astype(BF)
    rank = nn(asked_rel, before)
    row_count = nn(asked_rel, jnp.ones((128, 128), BF))
    earlier = onehot(iota((CTX_DEVS, CTX_DEVS), 1) < iota((CTX_DEVS, CTX_DEVS), 0))
    ahead = nn(earlier, row_count.astype(BF))
    place = asked_rel.astype(F32) * (ahead + rank + 1.0)
    place_row = jnp.sum(nn(place.astype(BF), slot) * holder, axis=0, keepdims=True)
    place_log = nt(log_lo, (log_hi.astype(F32) * place_row).astype(BF))
    looked = nn(place_log.astype(BF), sel_hi) * sel_lo.astype(F32)
    pos_sel = jnp.sum(looked, axis=0, keepdims=True)
    member = jnp.zeros((POOL, 128), F32)
    pool_id = iota((POOL, 128), 0).astype(F32) + 1.0
    for i in range(NSEL // 2):
        part = pos_sel[:, i * 128 : (i + 1) * 128]
        posn[i : i + 1, :] = part
        member = member + jnp.where(jnp.abs(pool_id - part) < 0.5, 1.0, 0.0)
    member = member + pltpu.roll(member, 64, 1)
    member = jnp.concatenate([member, jnp.zeros((128 - POOL, 128), F32)], axis=0).T[:Q_DEV, :]
    to_keys = onehot(iota((128, PART_KEYS), 0) == (iota((128, PART_KEYS), 1) >> 4))
    bias[...] = jnp.where(nn(member.astype(BF), to_keys) > 0.5, 0.0, NEG)

    count_lane = nt(jnp.ones((8, 128), BF), asked_rel)
    ahead_lane = nn(
        count_lane.astype(BF), onehot(iota((CTX_DEVS, CTX_DEVS), 0) < iota((CTX_DEVS, CTX_DEVS), 1))
    )
    count_lane = count_lane[0:1, :]
    ahead_lane = ahead_lane[0:1, :]
    lane_of = onehot(iota((CTX_DEVS, PART_KEYS), 0) == (iota((CTX_DEVS, PART_KEYS), 1) >> 4))
    pool_row = iota((POOL, CTX_DEVS), 0).astype(F32)
    for k, pack in ((0, pack0), (1, pack1)):
        hit = (jnp.abs(ahead_lane + float(k) - pool_row) < 0.5) & (count_lane > k + 0.5)
        pack[...] = nn(onehot(hit), lane_of)

    top[...] = jnp.full(top.shape, NEG, F32)
    total[...] = jnp.zeros(total.shape, F32)
    acc[...] = jnp.zeros(acc.shape, F32)

    @pl.loop(1, CTX_DEVS)
    def _(s):
        block_copy(s).wait_recv()

    def direct(way, half, what):
        ref = (kv, rp)[what]
        return pltpu.make_async_remote_copy(
            src_ref=ref.at[y, half],
            dst_ref=ref.at[y, half],
            send_sem=ag_send.at[way, half, what],
            recv_sem=ag_recv.at[way, half, what],
            device_id=head_peer((1, 3)[way]),
            device_id_type=MESH,
        )

    def forward(way, what):
        ref = (kv, rp)[what]
        origin = lax.rem(y + (3, 1)[way], HEAD_DEVS)
        return pltpu.make_async_remote_copy(
            src_ref=ref.at[origin, way],
            dst_ref=ref.at[origin, way],
            send_sem=fw_send.at[way, what],
            recv_sem=fw_recv.at[way, what],
            device_id=head_peer((1, 3)[way]),
            device_id_type=MESH,
        )

    dup = onehot((iota((128, 128), 0) & 63) == (iota((128, 128), 1) & 63))
    low = iota((1, 128), 1) < ROPE
    for half in range(2):
        same_row = iota((1, PART, PART_KEYS), 1) == (iota((1, PART, PART_KEYS), 2) & (PART - 1))
        compact = []
        for pack in (pack0, pack1):
            wide = jnp.where(same_row, pack[half * 32 : half * 32 + 32, :][:, None, :], 0.0)
            compact.append(wide.reshape(HALF, PART_KEYS).astype(BF))
        flat = recv[...].reshape(PART_KEYS, PAIR)
        kv[y, half] = (
            nn(compact[0], flat[:, 0:512]) + nn(compact[1], flat[:, 512:1024])
        ).astype(BF)
        ropes = flat[:, 1280:1408]
        ropes0 = jnp.where(low, ropes, jnp.zeros_like(ropes))
        ropes1 = jnp.where(low, jnp.zeros_like(ropes), ropes)
        twice = nn(
            (nn(compact[0], ropes0) + nn(compact[1], ropes1)).astype(BF), dup
        ).astype(BF)
        rp[y, half] = jnp.where(low, twice[: HALF // 2], twice[HALF // 2 :])
        for way in range(2):
            for what in range(2):
                direct(way, half, what).start()
        ukeys[half * HALF : half * HALF + HALF, :] = (
            nn(compact[0], flat[:, 1024:1152]) + nn(compact[1], flat[:, 1152:1280])
        ).astype(BF)

    for d in range(1, HEAD_DEVS):
        iq_copy(d).wait_recv()
        iw_copy(d).wait_recv()

    @pl.loop(0, 4)
    def _(i):
        keys_at = pl.ds(pl.multiple_of(i * 256, 256), 256)
        keys = ukeys[keys_at, :]

        def heads(j, sums):
            part = lax.div(j, 4)
            quad = lax.rem(j, 4)
            queries = iq_all[part, pl.ds(pl.multiple_of(quad * 256, 256), 256), :]
            raw = jnp.maximum(nt(keys, queries), 0.0)
            return (
                sums
                + raw[:, :128] * iw_all[part, pl.ds(quad * 2, 1), :]
                + raw[:, 128:] * iw_all[part, pl.ds(quad * 2 + 1, 1), :]
            )

        sums = lax.fori_loop(0, 16, heads, jnp.zeros((256, 128), F32))
        wsum[pl.ds(pl.multiple_of(i * 16, 16), 16)] = (sums + pltpu.roll(sums, 64, 1)).reshape(
            16, PART, 128
        )

    @pl.loop(0, NSEL // 2)
    def _(i):
        at = posn[pl.ds(i, 1), :] - 1.0
        ids = iota((POOL, PART, 128), 0).astype(F32)
        chosen = jnp.where(jnp.abs(ids - at[None]) < 0.5, wsum[...], 0.0)
        picked[i] = jnp.sum(chosen, axis=0)

    def picked_copy(d):
        to = lax.rem(y + d, HEAD_DEVS)
        return pltpu.make_async_remote_copy(
            src_ref=picked.at[pl.ds(to * 4, 4)],
            dst_ref=picked_in.at[y],
            send_sem=pk_send.at[d - 1],
            recv_sem=pk_recv.at[d - 1],
            device_id=head_peer(d),
            device_id_type=MESH,
        )

    for d in range(1, HEAD_DEVS):
        picked_copy(d).start()
    picked_in[y] = picked[pl.ds(y * 4, 4)]

    factor = (HEAD_DIM + ROPE) ** -0.5 * 1.4426950408889634

    @pl.loop(0, 8)
    def _(step):
        for k, way, half in ((2, 0, 0), (3, 1, 0), (4, 0, 1), (5, 1, 1)):

            @pl.when(step == k)
            def _():
                for what in range(2):
                    direct(way, half, what).wait_recv()
                    if way == half:
                        forward(way, what).start()

        for k, way in ((6, 0), (7, 1)):

            @pl.when(step == k)
            def _():
                for what in range(2):
                    forward(way, what).wait_recv()

        side = jnp.where(lax.rem(step, 2) == 0, 3, 1)
        ahead_y = jnp.where(step < 2, 0, jnp.where(step < 6, side, 2))
        origin = lax.rem(y + ahead_y, HEAD_DEVS)
        half = jnp.where(
            step < 2, step, jnp.where(step < 6, lax.div(step - 2, 2), step - 6)
        )

        @pl.loop(0, 4)
        def _(g):
            at = pl.ds(pl.multiple_of(g * 256, 256), 256)
            keys = kv[origin, half]
            ropes = rp[origin, half]
            scores = nt(qlat[at, :], keys)
            scores = scores + jnp.concatenate([nt(qra[at, :], ropes), nt(qrb[at, :], ropes)], axis=1)
            masked = bias[:, pl.ds(pl.multiple_of(half * HALF, HALF), HALF)]
            scores = (scores.reshape(4, Q_DEV, HALF) + masked[None]).reshape(256, HALF)
            old = top[at, :]
            new = jnp.maximum(old, jnp.max(scores, axis=1, keepdims=True))
            expo = jnp.exp2((scores - new) * factor)
            keep = jnp.exp2((old - new) * factor)
            total[at, :] = total[at, :] * keep + jnp.sum(expo, axis=1, keepdims=True)
            acc[at, :] = acc[at, :] * keep + nn(expo.astype(BF), keys)
            top[at, :] = new

    cp_wuv.wait()
    for h in range(HEADS_DEV):
        at = slice(h * Q_DEV, h * Q_DEV + Q_DEV)
        context = (acc[at, :] / total[at, :]).astype(BF)
        attn_ref[:, h * HEAD_DIM : (h + 1) * HEAD_DIM] = nn(context, wuv_v[h]).astype(BF)

    for d in range(1, HEAD_DEVS):
        picked_copy(d).wait_recv()
    for i in range(4):
        even = jnp.concatenate([picked_in[j, i] for j in range(HEAD_DEVS)], axis=0)
        both = jnp.concatenate([even, pltpu.roll(even, 64, 1)], axis=0)
        idx_ref[:, i * 128 : (i + 1) * 128] = both.T[:Q_DEV, :]

    @pl.loop(1, CTX_DEVS)
    def _(s):
        request(s).wait_send()
        block_copy(s).wait_send()

    for d in range(1, HEAD_DEVS):
        iq_copy(d).wait_send()
        iw_copy(d).wait_send()
        picked_copy(d).wait_send()
    for way in range(2):
        for what in range(2):
            for half in range(2):
                direct(way, half, what).wait_send()
            forward(way, what).wait_send()


def shards(
    query, w_uk, w_uv, index_query, index_weight, cache_rows, key_scale, selected, block_home
):
    vmem = pl.BlockSpec(memory_space=pltpu.VMEM)
    hbm = pl.BlockSpec(memory_space=pl.ANY)
    dma = pltpu.SemaphoreType.DMA
    width = cache_rows.shape[1]
    attn, idx = pl.pallas_call(
        kernel,
        out_shape=(
            jax.ShapeDtypeStruct((Q_DEV, HEADS_DEV * HEAD_DIM), BF),
            jax.ShapeDtypeStruct((Q_DEV, NSEL * BLOCK // HEAD_DEVS), F32),
        ),
        in_specs=[vmem] * 4 + [hbm] * 5,
        out_specs=(vmem, vmem),
        scratch_shapes=[
            pltpu.VMEM((BLK_DEV, PART, width), BF),
            pltpu.VMEM(query.shape, BF),
            pltpu.VMEM(index_query.shape, BF),
            pltpu.VMEM(w_uk.shape, BF),
            pltpu.VMEM(w_uv.shape, BF),
            pltpu.VMEM((CTX_DEVS, 1, 128), F32),
            pltpu.VMEM((CTX_DEVS, 1, 128), F32),
            pltpu.VMEM((BLK_DEV * PART, LATENT + 384), BF),
            pltpu.VMEM((2, CTX_DEVS, 512), F32),
            pltpu.VMEM((CTX_DEVS, PART, PAIR), BF),
            pltpu.VMEM((CTX_DEVS, PART, PAIR), BF),
            pltpu.VMEM((NSEL // 2, 128), F32),
            pltpu.VMEM((Q_DEV, PART_KEYS), F32),
            pltpu.VMEM((POOL, PART_KEYS), F32),
            pltpu.VMEM((POOL, PART_KEYS), F32),
            pltpu.VMEM((PART_KEYS, IDX_DIM), BF),
            pltpu.VMEM((HEAD_DEVS, 2, HALF, LATENT), BF),
            pltpu.VMEM((HEAD_DEVS, 2, HALF // 2, 128), BF),
            pltpu.VMEM((HEAD_DEVS, ROWS, IDX_DIM), BF),
            pltpu.VMEM((HEAD_DEVS, 8, 128), F32),
            pltpu.VMEM((ROWS, LATENT), BF),
            pltpu.VMEM((ROWS, 128), BF),
            pltpu.VMEM((ROWS, 128), BF),
            pltpu.VMEM((POOL, PART, 128), F32),
            pltpu.VMEM((NSEL // 2, PART, 128), F32),
            pltpu.VMEM((HEAD_DEVS, NSEL // 8, PART, 128), F32),
            pltpu.VMEM((ROWS, 1), F32),
            pltpu.VMEM((ROWS, 1), F32),
            pltpu.VMEM((ROWS, LATENT), F32),
            dma((5,)),
            dma((CTX_DEVS,)),
            dma((CTX_DEVS,)),
            dma((CTX_DEVS,)),
            dma((CTX_DEVS,)),
            dma((3,)),
            dma((3,)),
            dma((3,)),
            dma((3,)),
            dma((3,)),
            dma((3,)),
            dma((2, 2, 2)),
            dma((2, 2, 2)),
            dma((2, 2)),
            dma((2, 2)),
        ],
        compiler_params=pltpu.CompilerParams(
            collective_id=0, has_side_effects=True, vmem_limit_bytes=58 * 1024 * 1024
        ),
    )(
        selected.T.reshape(1, Q_DEV * NSEL),
        block_home.reshape(1, NBLK),
        key_scale.reshape(BLK_DEV, BLOCK),
        index_weight.T.reshape(8, 128),
        query,
        index_query,
        cache_rows.reshape(BLK_DEV, BLOCK, width),
        w_uk,
        w_uv,
    )
    return (attn.reshape(Q_DEV, HEADS_DEV, HEAD_DIM), idx)


def solution(mesh):
    return jax.shard_map(
        shards,
        mesh=mesh,
        in_specs=(
            P("ctx", "head", None),
            P("head", None, None),
            P("head", None, None),
            P("ctx", "head", None),
            P("ctx", "head"),
            P("ctx", None),
            P("ctx"),
            P("ctx", None),
            P(),
        ),
        out_specs=(P("ctx", "head", None), P("ctx", "head")),
        check_vma=False,
    )
```

```python
import jax
import jax.numpy as jnp
from jax import lax
from jax.experimental import pallas as pl
from jax.experimental.pallas import tpu as pltpu
from jax.sharding import PartitionSpec as P

LATENT = 512
ROPE = 64
HEAD_DIM = 128
IDX_DIM = 128
BLOCK = 64
NSEL = 32
POOL = 64
BLK_DEV = 32
NBLK = 2048
Q_DEV = 64
HEADS_DEV = 16
CTX_DEVS = 64
HEAD_DEVS = 4
PART = BLOCK // HEAD_DEVS
ROWS = HEADS_DEV * Q_DEV
PART_KEYS = POOL * PART
PARTS = 4
PIECE = PART_KEYS // PARTS
PAIR = 2 * LATENT + 2 * IDX_DIM + 2 * ROPE
NEG = -1e30
MESH = pl.DeviceIdType.MESH
BF = jnp.bfloat16
F32 = jnp.float32


def nn(a, b):
    return jnp.dot(a, b, preferred_element_type=F32)


def nt(a, b):
    return lax.dot_general(a, b, (((1,), (1,)), ((), ())), preferred_element_type=F32)


def iota(shape, dim):
    return lax.broadcasted_iota(jnp.int32, shape, dim)


def onehot(cond):
    return jnp.where(cond, 1.0, 0.0).astype(BF)


def kernel(
    sel_ref,
    home_ref,
    scale_ref,
    iw_ref,
    query_hbm,
    iq_hbm,
    cache_hbm,
    wuk_hbm,
    wuv_hbm,
    attn_ref,
    idx_ref,
    cache_v,
    query_v,
    iq_v,
    wuk_v,
    wuv_v,
    wuv_t,
    want,
    want_in,
    weights,
    expand,
    served,
    recv,
    posn,
    bias,
    pack0,
    pack1,
    kv,
    rp,
    iq_all,
    iw_all,
    qlat,
    qra,
    qrb,
    wsum,
    picked,
    picked_in,
    top,
    total,
    acc,
    local_sem,
    req_send,
    req_recv,
    blk_send,
    blk_recv,
    iq_send,
    iq_recv,
    iw_send,
    iw_recv,
    pk_send,
    pk_recv,
    ag_send,
    ag_recv,
    fw_send,
    fw_recv,
):
    me = lax.axis_index("ctx")
    y = lax.axis_index("head")

    def ctx_peer(c):
        return (lax.rem(c + 2 * CTX_DEVS, CTX_DEVS), y)

    def head_peer(d):
        return (me, lax.rem(y + d, HEAD_DEVS))

    barrier = pltpu.get_barrier_semaphore()

    @pl.loop(1, CTX_DEVS)
    def _(s):
        pl.semaphore_signal(barrier, inc=1, device_id=ctx_peer(me + s), device_id_type=MESH)

    for d in range(1, HEAD_DEVS):
        pl.semaphore_signal(barrier, inc=1, device_id=head_peer(d), device_id_type=MESH)

    cp_cache = pltpu.make_async_copy(cache_hbm, cache_v, local_sem.at[0])
    cp_query = pltpu.make_async_copy(query_hbm, query_v, local_sem.at[1])
    cp_iq = pltpu.make_async_copy(iq_hbm, iq_v, local_sem.at[2])
    cp_wuk = pltpu.make_async_copy(wuk_hbm, wuk_v, local_sem.at[3])
    cp_wuv = pltpu.make_async_copy(wuv_hbm, wuv_v, local_sem.at[4])
    for cp in (cp_cache, cp_query, cp_iq, cp_wuk, cp_wuv):
        cp.start()

    sel = jnp.concatenate([sel_ref[i : i + 1, :] for i in range(NSEL)], axis=1)
    home = home_ref[...]
    sel_hi = onehot(iota((32, NBLK), 0) == (sel >> 6))
    sel_lo = onehot(iota((64, NBLK), 0) == (sel & 63))
    lane = iota((1, NBLK), 1)
    log_hi = onehot(iota((32, NBLK), 0) == (lane >> 6))
    log_lo = onehot(iota((64, NBLK), 0) == (lane & 63))
    counts = nt(sel_hi, sel_lo)
    wanted = onehot(counts > 0.5)
    wanted_row = jnp.sum(nn(wanted, log_lo) * log_hi.astype(F32), axis=0, keepdims=True)
    rel = (me - (home >> 5)) & (CTX_DEVS - 1)
    holder = jnp.where(iota((CTX_DEVS, NBLK), 0) == rel, 1.0, 0.0)
    slot = onehot(iota((128, NBLK), 0) == (home & (BLK_DEV - 1)))
    want_rel = nt((holder * wanted_row).astype(BF), slot)
    want[...] = want_rel.reshape(CTX_DEVS, 1, 128)
    want_in[0] = want[0]

    pl.semaphore_wait(barrier, CTX_DEVS - 1 + HEAD_DEVS - 1)

    def request(s):
        return pltpu.make_async_remote_copy(
            src_ref=want.at[s],
            dst_ref=want_in.at[s],
            send_sem=req_send.at[s],
            recv_sem=req_recv.at[s],
            device_id=ctx_peer(me - s),
            device_id_type=MESH,
        )

    @pl.loop(1, CTX_DEVS)
    def _(s):
        request(s).start()

    cp_cache.wait()
    row = iota((BLK_DEV * PART, NBLK), 0)
    mine = onehot(iota((BLK_DEV * PART, NBLK), 1) == (row >> 4) * BLOCK + y * PART + (row & 15))
    scaled = (cache_v[LATENT + ROPE :, :].astype(F32) * scale_ref[...]).astype(BF)
    rope = cache_v[LATENT : LATENT + ROPE, :]
    weights[:, :LATENT] = nt(mine, cache_v[:LATENT, :]).astype(BF)
    weights[:, LATENT : LATENT + IDX_DIM] = nt(mine, scaled).astype(BF)
    ropes = nt(mine, jnp.concatenate([rope, rope], axis=0)).astype(BF)
    low = iota((1, 128), 1) < ROPE
    weights[:, LATENT + 128 : LATENT + 256] = jnp.where(low, ropes, jnp.zeros_like(ropes))
    weights[:, LATENT + 256 :] = jnp.where(low, jnp.zeros_like(ropes), ropes)

    @pl.loop(1, CTX_DEVS)
    def _(s):
        request(s).wait_recv()

    asked = want_in[...].reshape(CTX_DEVS, 128)
    before = onehot(iota((128, 128), 0) < iota((128, 128), 1))
    order = nn(asked.astype(BF), before)
    spread = onehot(iota((128, 512), 0) == (iota((128, 512), 1) >> 4))
    for k in range(2):
        first = jnp.where(jnp.abs(order - float(k)) < 0.5, asked, 0.0)
        expand[k] = nn(first.astype(BF), spread)

    def block_copy(s):
        return pltpu.make_async_remote_copy(
            src_ref=served.at[s],
            dst_ref=recv.at[s],
            send_sem=blk_send.at[s],
            recv_sem=blk_recv.at[s],
            device_id=ctx_peer(me + s),
            device_id_type=MESH,
        )

    group = 16

    @pl.loop(0, CTX_DEVS // group)
    def _(i):
        at = pl.ds(pl.multiple_of(i * group, group), group)
        same_row = iota((1, PART, 512), 1) == (iota((1, PART, 512), 2) & (PART - 1))
        gather = []
        for k in range(2):
            wide = jnp.where(same_row, expand[k, at, :][:, None, :], 0.0)
            gather.append(wide.reshape(group * PART, 512).astype(BF))
        o0 = nn(gather[0], weights[:, : LATENT + 256]).astype(BF)
        o1 = nn(gather[1], weights[:, : LATENT + IDX_DIM]).astype(BF)
        r1 = nn(gather[1], weights[:, LATENT + 256 :]).astype(BF)
        shape = (group, PART, -1)
        served[at, :, 0:512] = o0[:, :512].reshape(shape)
        served[at, :, 512:1024] = o1[:, :512].reshape(shape)
        served[at, :, 1024:1152] = o0[:, 512:640].reshape(shape)
        served[at, :, 1152:1280] = o1[:, 512:640].reshape(shape)
        served[at, :, 1280:1408] = (o0[:, 640:768] + r1).reshape(shape)

        @pl.loop(jnp.where(i == 0, 1, 0), group)
        def _(j):
            block_copy(i * group + j).start()

    recv[0] = served[0]

    cp_query.wait()
    cp_iq.wait()
    cp_wuk.wait()
    cp_wuv.wait()
    col = iota((HEAD_DIM + ROPE, 384), 0)
    out = iota((HEAD_DIM + ROPE, 384), 1)
    q_arrange = onehot(
        ((out < 192) & (col == out)) | ((out >= 320) & (col == out - 320 + HEAD_DIM))
    )

    def by_head(g):
        rows_g = iota((256, ROWS), 0)
        want_row = (rows_g & (Q_DEV - 1)) * HEADS_DEV + g * 4 + (rows_g >> 6)
        return onehot(iota((256, ROWS), 1) == want_row)

    @pl.loop(0, 4)
    def _(g):
        at = pl.ds(pl.multiple_of(g * 256, 256), 256)
        iq_all[y, :, at] = nn(by_head(g), iq_v[...].reshape(ROWS, IDX_DIM)).astype(BF).T

    for i in range(HEADS_DEV // 2):
        pair = [iw_ref[2 * i + k : 2 * i + k + 1, :] for k in range(2)]
        iw_all[y, i : i + 1, :] = jnp.concatenate(pair, axis=1)

    def iq_copy(d):
        return pltpu.make_async_remote_copy(
            src_ref=iq_all.at[y],
            dst_ref=iq_all.at[y],
            send_sem=iq_send.at[d - 1],
            recv_sem=iq_recv.at[d - 1],
            device_id=head_peer(d),
            device_id_type=MESH,
        )

    def iw_copy(d):
        return pltpu.make_async_remote_copy(
            src_ref=iw_all.at[y],
            dst_ref=iw_all.at[y],
            send_sem=iw_send.at[d - 1],
            recv_sem=iw_recv.at[d - 1],
            device_id=head_peer(d),
            device_id_type=MESH,
        )

    for d in range(1, HEAD_DEVS):
        iq_copy(d).start()
        iw_copy(d).start()

    @pl.loop(0, 4)
    def _(g):
        at = pl.ds(pl.multiple_of(g * 256, 256), 256)
        mine = nn(by_head(g), query_v[...].reshape(ROWS, HEAD_DIM + ROPE)).astype(BF)
        parts = nn(mine, q_arrange).astype(BF)
        lat = [nn(parts[k * 64 : k * 64 + 64, :HEAD_DIM], wuk_v[g * 4 + k]) for k in range(4)]
        qlat[:, at] = jnp.concatenate(lat, axis=0).astype(BF).T
        qra[:, at] = parts[:, 128:256].T
        qrb[:, at] = parts[:, 256:384].T

    @pl.loop(0, HEADS_DEV)
    def _(h):
        wuv_t[h] = wuv_v[h].T

    asked_rel = want[...].reshape(CTX_DEVS, 128).astype(BF)
    rank = nn(asked_rel, before)
    row_count = nn(asked_rel, jnp.ones((128, 128), BF))
    earlier = onehot(iota((CTX_DEVS, CTX_DEVS), 1) < iota((CTX_DEVS, CTX_DEVS), 0))
    ahead = nn(earlier, row_count.astype(BF))
    place = asked_rel.astype(F32) * (ahead + rank + 1.0)
    place_row = jnp.sum(nn(place.astype(BF), slot) * holder, axis=0, keepdims=True)
    place_log = nt(log_lo, (log_hi.astype(F32) * place_row).astype(BF))
    looked = nn(place_log.astype(BF), sel_hi) * sel_lo.astype(F32)
    pos_sel = jnp.sum(looked, axis=0, keepdims=True)
    member = jnp.zeros((POOL, 128), F32)
    pool_id = iota((POOL, 128), 0).astype(F32) + 1.0
    for i in range(NSEL // 2):
        part = pos_sel[:, i * 128 : (i + 1) * 128]
        posn[i : i + 1, :] = part
        member = member + jnp.where(jnp.abs(pool_id - part) < 0.5, 1.0, 0.0)
    member = member + pltpu.roll(member, 64, 1)
    allowed = jnp.broadcast_to(member[:, None, :], (POOL, PART, 128)).reshape(PART_KEYS, 128)
    bias[...] = jnp.where(allowed > 0.5, 0.0, NEG)

    count_lane = nt(jnp.ones((8, 128), BF), asked_rel)
    ahead_lane = nn(
        count_lane.astype(BF), onehot(iota((CTX_DEVS, CTX_DEVS), 0) < iota((CTX_DEVS, CTX_DEVS), 1))
    )
    count_lane = count_lane[0:1, :]
    ahead_lane = ahead_lane[0:1, :]
    lane_of = onehot(iota((CTX_DEVS, PART_KEYS), 0) == (iota((CTX_DEVS, PART_KEYS), 1) >> 4))
    pool_row = iota((POOL, CTX_DEVS), 0).astype(F32)
    for k, pack in ((0, pack0), (1, pack1)):
        hit = (jnp.abs(ahead_lane + float(k) - pool_row) < 0.5) & (count_lane > k + 0.5)
        pack[...] = nn(onehot(hit), lane_of)

    top[...] = jnp.full(top.shape, NEG, F32)
    total[...] = jnp.zeros(total.shape, F32)
    acc[...] = jnp.zeros(acc.shape, F32)

    def direct(way, part, what):
        ref, size = ((kv, PIECE), (rp, PIECE // 2))[what]
        at = ref.at[y, pl.ds(part * size, size)]
        return pltpu.make_async_remote_copy(
            src_ref=at,
            dst_ref=at,
            send_sem=ag_send.at[way, part, what],
            recv_sem=ag_recv.at[way, part, what],
            device_id=head_peer((1, 3)[way]),
            device_id_type=MESH,
        )

    def forward(way, part, what):
        ref, size = ((kv, PIECE), (rp, PIECE // 2))[what]
        origin = lax.rem(y + (3, 1)[way], HEAD_DEVS)
        at = ref.at[origin, pl.ds(part * size + way * (size // 2), size // 2)]
        return pltpu.make_async_remote_copy(
            src_ref=at,
            dst_ref=at,
            send_sem=fw_send.at[way, part, what],
            recv_sem=fw_recv.at[way, part, what],
            device_id=head_peer((1, 3)[way]),
            device_id_type=MESH,
        )

    dup = onehot((iota((128, 128), 0) & 63) == (iota((128, 128), 1) & 63))

    def compact(part):
        blocks = 32 + 8 * (part + 1)
        depth = blocks * PART
        at = slice(part * 16, part * 16 + 16)
        same_row = iota((1, PART, depth), 1) == (iota((1, PART, depth), 2) & (PART - 1))
        move = []
        for pack in (pack0, pack1):
            wide = jnp.where(same_row, pack[at, :depth][:, None, :], 0.0)
            move.append(wide.reshape(PIECE, depth).astype(BF))
        flat = recv[:blocks].reshape(depth, PAIR)
        kv[y, part * PIECE : part * PIECE + PIECE, :] = (
            nn(move[0], flat[:, 0:512]) + nn(move[1], flat[:, 512:1024])
        ).astype(BF)
        ropes = flat[:, 1280:1408]
        ropes0 = jnp.where(low, ropes, jnp.zeros_like(ropes))
        ropes1 = jnp.where(low, jnp.zeros_like(ropes), ropes)
        twice = nn((nn(move[0], ropes0) + nn(move[1], ropes1)).astype(BF), dup).astype(BF)
        rp[y, part * (PIECE // 2) : (part + 1) * (PIECE // 2), :] = jnp.where(
            low, twice[: PIECE // 2], twice[PIECE // 2 :]
        )
        for way in range(2):
            for what in range(2):
                direct(way, part, what).start()
        return (nn(move[0], flat[:, 1024:1152]) + nn(move[1], flat[:, 1152:1280])).astype(BF)

    def pass_on(part):
        for way in range(2):
            for what in range(2):
                direct(way, part, what).wait_recv()
                forward(way, part, what).start()

    def index(part, keys):
        def heads(j, sums):
            raw = jnp.maximum(nn(keys, iq_all[j]), 0.0)
            for i in range(8):
                sums = sums + raw[:, i * 128 : i * 128 + 128] * iw_all[j, i : i + 1, :]
            return sums

        sums = lax.fori_loop(0, HEAD_DEVS, heads, jnp.zeros((PIECE, 128), F32))
        wsum[part * 16 : part * 16 + 16] = (sums + pltpu.roll(sums, 64, 1)).reshape(16, PART, 128)

    factor = (HEAD_DIM + ROPE) ** -0.5 * 1.4426950408889634

    def attend(*pieces):
        keys, scores, masks = [], [], []
        for ahead_y, part in pieces:
            origin = lax.rem(y + ahead_y, HEAD_DEVS)
            keys.append(kv[origin, part * PIECE : part * PIECE + PIECE, :])
            ropes = rp[origin, part * (PIECE // 2) : (part + 1) * (PIECE // 2), :]
            scores += [nn(ropes, qra[...]), nn(ropes, qrb[...])]
            masks.append(bias[part * PIECE : part * PIECE + PIECE, :])
        keys = jnp.concatenate(keys, axis=0)
        mask = jnp.concatenate(masks, axis=0)
        scores = nn(keys, qlat[...]) + jnp.concatenate(scores, axis=0)
        scores = scores + jnp.concatenate([mask] * (ROWS // 128), axis=1)
        old = top[...]
        new = jnp.maximum(old, jnp.max(scores, axis=0, keepdims=True))
        expo = jnp.exp2((scores - new) * factor)
        keep = jnp.exp2((old - new) * factor)
        total[...] = total[...] * keep + jnp.sum(expo, axis=0, keepdims=True)
        acc[...] = acc[...] * keep + nn(keys.T, expo.astype(BF))
        top[...] = new

    def arrived(first, last):
        @pl.loop(first, last)
        def _(s):
            block_copy(s).wait_recv()

    arrived(1, 40)
    keys = compact(0)
    for d in range(1, HEAD_DEVS):
        iq_copy(d).wait_recv()
        iw_copy(d).wait_recv()
    index(0, keys)
    attend((0, 0))

    arrived(40, 48)
    keys = compact(1)
    pass_on(0)
    index(1, keys)
    attend((0, 1), (3, 0), (1, 0))

    arrived(48, 56)
    keys = compact(2)
    pass_on(1)
    index(2, keys)
    for way in range(2):
        for what in range(2):
            forward(way, 0, what).wait_recv()
    attend((0, 2), (2, 0))
    attend((3, 1), (1, 1))

    arrived(56, 64)
    keys = compact(3)
    pass_on(2)
    index(3, keys)

    @pl.loop(0, NSEL // 2)
    def _(i):
        at = posn[pl.ds(i, 1), :] - 1.0
        ids = iota((POOL, PART, 128), 0).astype(F32)
        chosen = jnp.where(jnp.abs(ids - at[None]) < 0.5, wsum[...], 0.0)
        picked[i] = jnp.sum(chosen, axis=0)

    def picked_copy(d):
        to = lax.rem(y + d, HEAD_DEVS)
        return pltpu.make_async_remote_copy(
            src_ref=picked.at[pl.ds(to * 4, 4)],
            dst_ref=picked_in.at[y],
            send_sem=pk_send.at[d - 1],
            recv_sem=pk_recv.at[d - 1],
            device_id=head_peer(d),
            device_id_type=MESH,
        )

    for d in range(1, HEAD_DEVS):
        picked_copy(d).start()
    picked_in[y] = picked[pl.ds(y * 4, 4)]

    for way in range(2):
        for what in range(2):
            forward(way, 1, what).wait_recv()
    attend((0, 3), (2, 1))
    attend((3, 2), (1, 2))
    pass_on(3)
    for way in range(2):
        for what in range(2):
            forward(way, 2, what).wait_recv()
    attend((2, 2), (3, 3), (1, 3))
    for way in range(2):
        for what in range(2):
            forward(way, 3, what).wait_recv()
    attend((2, 3))

    for m in range(HEADS_DEV // 2):
        at = slice(m * 128, m * 128 + 128)
        context = (acc[:, at] / total[:, at]).astype(BF)
        both = nn(wuv_t[2 * m : 2 * m + 2].reshape(256, LATENT), context)
        joined = jnp.where(low, both[:128], both[128:]).T
        attn_ref[:, 2 * m * HEAD_DIM : (2 * m + 1) * HEAD_DIM] = joined[:Q_DEV].astype(BF)
        attn_ref[:, (2 * m + 1) * HEAD_DIM : (2 * m + 2) * HEAD_DIM] = joined[Q_DEV:].astype(BF)

    for d in range(1, HEAD_DEVS):
        picked_copy(d).wait_recv()
    for i in range(4):
        even = jnp.concatenate([picked_in[j, i] for j in range(HEAD_DEVS)], axis=0)
        both = jnp.concatenate([even, pltpu.roll(even, 64, 1)], axis=0)
        idx_ref[:, i * 128 : (i + 1) * 128] = both.T[:Q_DEV, :]

    @pl.loop(1, CTX_DEVS)
    def _(s):
        request(s).wait_send()
        block_copy(s).wait_send()

    for d in range(1, HEAD_DEVS):
        iq_copy(d).wait_send()
        iw_copy(d).wait_send()
        picked_copy(d).wait_send()
    for way in range(2):
        for what in range(2):
            for part in range(PARTS):
                direct(way, part, what).wait_send()
                forward(way, part, what).wait_send()


def shards(
    query, w_uk, w_uv, index_query, index_weight, cache_rows, key_scale, selected, block_home
):
    vmem = pl.BlockSpec(memory_space=pltpu.VMEM)
    hbm = pl.BlockSpec(memory_space=pl.ANY)
    dma = pltpu.SemaphoreType.DMA
    width = cache_rows.shape[1]
    attn, idx = pl.pallas_call(
        kernel,
        out_shape=(
            jax.ShapeDtypeStruct((Q_DEV, HEADS_DEV * HEAD_DIM), BF),
            jax.ShapeDtypeStruct((Q_DEV, NSEL * BLOCK // HEAD_DEVS), F32),
        ),
        in_specs=[vmem] * 4 + [hbm] * 5,
        out_specs=(vmem, vmem),
        scratch_shapes=[
            pltpu.VMEM((width, BLK_DEV * BLOCK), BF),
            pltpu.VMEM(query.shape, BF),
            pltpu.VMEM(index_query.shape, BF),
            pltpu.VMEM(w_uk.shape, BF),
            pltpu.VMEM(w_uv.shape, BF),
            pltpu.VMEM((HEADS_DEV, HEAD_DIM, LATENT), BF),
            pltpu.VMEM((CTX_DEVS, 1, 128), F32),
            pltpu.VMEM((CTX_DEVS, 1, 128), F32),
            pltpu.VMEM((BLK_DEV * PART, LATENT + 384), BF),
            pltpu.VMEM((2, CTX_DEVS, 512), F32),
            pltpu.VMEM((CTX_DEVS, PART, PAIR), BF),
            pltpu.VMEM((CTX_DEVS, PART, PAIR), BF),
            pltpu.VMEM((NSEL // 2, 128), F32),
            pltpu.VMEM((PART_KEYS, 128), F32),
            pltpu.VMEM((POOL, PART_KEYS), F32),
            pltpu.VMEM((POOL, PART_KEYS), F32),
            pltpu.VMEM((HEAD_DEVS, PART_KEYS, LATENT), BF),
            pltpu.VMEM((HEAD_DEVS, PART_KEYS // 2, 128), BF),
            pltpu.VMEM((HEAD_DEVS, IDX_DIM, ROWS), BF),
            pltpu.VMEM((HEAD_DEVS, 8, 128), F32),
            pltpu.VMEM((LATENT, ROWS), BF),
            pltpu.VMEM((128, ROWS), BF),
            pltpu.VMEM((128, ROWS), BF),
            pltpu.VMEM((POOL, PART, 128), F32),
            pltpu.VMEM((NSEL // 2, PART, 128), F32),
            pltpu.VMEM((HEAD_DEVS, NSEL // 8, PART, 128), F32),
            pltpu.VMEM((1, ROWS), F32),
            pltpu.VMEM((1, ROWS), F32),
            pltpu.VMEM((LATENT, ROWS), F32),
            dma((5,)),
            dma((CTX_DEVS,)),
            dma((CTX_DEVS,)),
            dma((CTX_DEVS,)),
            dma((CTX_DEVS,)),
            dma((3,)),
            dma((3,)),
            dma((3,)),
            dma((3,)),
            dma((3,)),
            dma((3,)),
            dma((2, PARTS, 2)),
            dma((2, PARTS, 2)),
            dma((2, PARTS, 2)),
            dma((2, PARTS, 2)),
        ],
        compiler_params=pltpu.CompilerParams(
            collective_id=0, has_side_effects=True, vmem_limit_bytes=58 * 1024 * 1024
        ),
    )(
        selected.T,
        block_home.reshape(1, NBLK),
        key_scale.reshape(1, BLK_DEV * BLOCK),
        index_weight.T,
        query,
        index_query,
        cache_rows.T,
        w_uk,
        w_uv,
    )
    return (attn.reshape(Q_DEV, HEADS_DEV, HEAD_DIM), idx)


def solution(mesh):
    return jax.shard_map(
        shards,
        mesh=mesh,
        in_specs=(
            P("ctx", "head", None),
            P("head", None, None),
            P("head", None, None),
            P("ctx", "head", None),
            P("ctx", "head"),
            P("ctx", None),
            P("ctx"),
            P("ctx", None),
            P(),
        ),
        out_specs=(P("ctx", "head", None), P("ctx", "head")),
        check_vma=False,
    )
```

```python
import jax
import jax.numpy as jnp
from jax import lax
from jax.experimental import pallas as pl
from jax.experimental.pallas import tpu as pltpu
from jax.sharding import PartitionSpec as P

LATENT = 512
ROPE = 64
HEAD_DIM = 128
IDX_DIM = 128
BLOCK = 64
NSEL = 32
POOL = 64
BLK_DEV = 32
NBLK = 2048
Q_DEV = 64
HEADS_DEV = 16
CTX_DEVS = 64
HEAD_DEVS = 4
PART = BLOCK // HEAD_DEVS
ROWS = HEADS_DEV * Q_DEV
PART_KEYS = POOL * PART
PARTS = 4
PIECE = PART_KEYS // PARTS
PAIR = 2 * LATENT + 2 * IDX_DIM + 2 * ROPE
NEG = -1e30
MESH = pl.DeviceIdType.MESH
BF = jnp.bfloat16
F32 = jnp.float32


def nn(a, b):
    return jnp.dot(a, b, preferred_element_type=F32)


def nt(a, b):
    return lax.dot_general(a, b, (((1,), (1,)), ((), ())), preferred_element_type=F32)


def iota(shape, dim):
    return lax.broadcasted_iota(jnp.int32, shape, dim)


def onehot(cond):
    return jnp.where(cond, 1.0, 0.0).astype(BF)


def kernel(
    sel_ref,
    home_ref,
    scale_ref,
    iw_ref,
    query_hbm,
    iq_hbm,
    cache_hbm,
    wuk_hbm,
    wuv_hbm,
    attn_ref,
    idx_ref,
    cache_v,
    query_v,
    iq_v,
    wuk_v,
    wuv_v,
    wuv_t,
    want,
    want_in,
    weights,
    expand,
    served,
    recv,
    posn,
    bias,
    pack0,
    pack1,
    kv,
    rp,
    iq_all,
    iw_all,
    qlat,
    qra,
    qrb,
    wsum,
    picked,
    picked_in,
    top,
    total,
    acc,
    local_sem,
    req_send,
    req_recv,
    blk_send,
    blk_recv,
    iq_send,
    iq_recv,
    iw_send,
    iw_recv,
    pk_send,
    pk_recv,
    ag_send,
    ag_recv,
    fw_send,
    fw_recv,
):
    me = lax.axis_index("ctx")
    y = lax.axis_index("head")

    my_x, my_z, my_core = lax.div(me, 16), lax.rem(lax.div(me, 2), 8), lax.rem(me, 2)

    def ctx_peer(s, way):
        turn = lax.div(s, 8)
        odd = lax.rem(turn, 2)
        dz = odd * lax.div(turn + 1, 2) + (1 - odd) * lax.rem(8 - lax.div(turn, 2), 8)
        dx = lax.rem(lax.div(s, 2), 4)
        to_x = lax.rem(my_x + way * dx + 4, 4)
        to_z = lax.rem(my_z + way * dz + 8, 8)
        to_core = lax.rem(my_core + s, 2)
        return ((to_x * 8 + to_z) * 2 + to_core, y)

    def head_peer(d):
        return (me, lax.rem(y + d, HEAD_DEVS))

    barrier = pltpu.get_barrier_semaphore()

    @pl.loop(1, CTX_DEVS)
    def _(s):
        pl.semaphore_signal(barrier, inc=1, device_id=ctx_peer(s, 1), device_id_type=MESH)

    for d in range(1, HEAD_DEVS):
        pl.semaphore_signal(barrier, inc=1, device_id=head_peer(d), device_id_type=MESH)

    cp_cache = pltpu.make_async_copy(cache_hbm, cache_v, local_sem.at[0])
    cp_query = pltpu.make_async_copy(query_hbm, query_v, local_sem.at[1])
    cp_iq = pltpu.make_async_copy(iq_hbm, iq_v, local_sem.at[2])
    cp_wuk = pltpu.make_async_copy(wuk_hbm, wuk_v, local_sem.at[3])
    cp_wuv = pltpu.make_async_copy(wuv_hbm, wuv_v, local_sem.at[4])
    cp_cache.start()

    sel = jnp.concatenate([sel_ref[i : i + 1, :] for i in range(NSEL)], axis=1)
    home = home_ref[...]
    sel_hi = onehot(iota((32, NBLK), 0) == (sel >> 6))
    sel_lo = onehot(iota((64, NBLK), 0) == (sel & 63))
    lane = iota((1, NBLK), 1)
    log_hi = onehot(iota((32, NBLK), 0) == (lane >> 6))
    log_lo = onehot(iota((64, NBLK), 0) == (lane & 63))
    counts = nt(sel_hi, sel_lo)
    wanted = onehot(counts > 0.5)
    wanted_row = jnp.sum(nn(wanted, log_lo) * log_hi.astype(F32), axis=0, keepdims=True)
    owner = home >> 5
    dz = (my_z - ((owner >> 1) & 7)) & 7
    turn = jnp.where(dz == 0, 0, jnp.where(dz <= 4, 2 * dz - 1, 16 - 2 * dz))
    rel = turn * 8 + ((my_x - (owner >> 4)) & 3) * 2 + ((my_core - owner) & 1)
    holder = jnp.where(iota((CTX_DEVS, NBLK), 0) == rel, 1.0, 0.0)
    slot = onehot(iota((128, NBLK), 0) == (home & (BLK_DEV - 1)))
    want_rel = nt((holder * wanted_row).astype(BF), slot)
    want[...] = want_rel.reshape(CTX_DEVS, 1, 128)
    want_in[0] = want[0]

    pl.semaphore_wait(barrier, CTX_DEVS - 1 + HEAD_DEVS - 1)

    def request(s):
        return pltpu.make_async_remote_copy(
            src_ref=want.at[s],
            dst_ref=want_in.at[s],
            send_sem=req_send.at[s],
            recv_sem=req_recv.at[s],
            device_id=ctx_peer(s, -1),
            device_id_type=MESH,
        )

    @pl.loop(1, CTX_DEVS)
    def _(s):
        request(s).start()

    cp_cache.wait()
    for cp in (cp_query, cp_iq, cp_wuk, cp_wuv):
        cp.start()
    row = iota((BLK_DEV * PART, NBLK), 0)
    mine = onehot(iota((BLK_DEV * PART, NBLK), 1) == (row >> 4) * BLOCK + y * PART + (row & 15))
    scaled = (cache_v[LATENT + ROPE :, :].astype(F32) * scale_ref[...]).astype(BF)
    rope = cache_v[LATENT : LATENT + ROPE, :]
    weights[:, :LATENT] = nt(mine, cache_v[:LATENT, :]).astype(BF)
    weights[:, LATENT : LATENT + IDX_DIM] = nt(mine, scaled).astype(BF)
    ropes = nt(mine, jnp.concatenate([rope, rope], axis=0)).astype(BF)
    low = iota((1, 128), 1) < ROPE
    weights[:, LATENT + 128 : LATENT + 256] = jnp.where(low, ropes, jnp.zeros_like(ropes))
    weights[:, LATENT + 256 :] = jnp.where(low, jnp.zeros_like(ropes), ropes)

    @pl.loop(1, CTX_DEVS)
    def _(s):
        request(s).wait_recv()

    asked = want_in[...].reshape(CTX_DEVS, 128)
    before = onehot(iota((128, 128), 0) < iota((128, 128), 1))
    order = nn(asked.astype(BF), before)
    spread = onehot(iota((128, 512), 0) == (iota((128, 512), 1) >> 4))
    for k in range(2):
        first = jnp.where(jnp.abs(order - float(k)) < 0.5, asked, 0.0)
        expand[k] = nn(first.astype(BF), spread)

    def block_copy(s):
        return pltpu.make_async_remote_copy(
            src_ref=served.at[s],
            dst_ref=recv.at[s],
            send_sem=blk_send.at[s],
            recv_sem=blk_recv.at[s],
            device_id=ctx_peer(s, 1),
            device_id_type=MESH,
        )

    group = 16

    @pl.loop(0, CTX_DEVS // group)
    def _(i):
        at = pl.ds(pl.multiple_of(i * group, group), group)
        same_row = iota((1, PART, 512), 1) == (iota((1, PART, 512), 2) & (PART - 1))
        gather = []
        for k in range(2):
            wide = jnp.where(same_row, expand[k, at, :][:, None, :], 0.0)
            gather.append(wide.reshape(group * PART, 512).astype(BF))
        o0 = nn(gather[0], weights[:, : LATENT + 256]).astype(BF)
        o1 = nn(gather[1], weights[:, : LATENT + IDX_DIM]).astype(BF)
        r1 = nn(gather[1], weights[:, LATENT + 256 :]).astype(BF)
        shape = (group, PART, -1)
        served[at, :, 0:512] = o0[:, :512].reshape(shape)
        served[at, :, 512:1024] = o1[:, :512].reshape(shape)
        served[at, :, 1024:1152] = o0[:, 512:640].reshape(shape)
        served[at, :, 1152:1280] = o1[:, 512:640].reshape(shape)
        served[at, :, 1280:1408] = (o0[:, 640:768] + r1).reshape(shape)

        @pl.loop(jnp.where(i == 0, 1, 0), group)
        def _(j):
            block_copy(i * group + j).start()

    recv[0] = served[0]

    cp_query.wait()
    cp_iq.wait()
    cp_wuk.wait()
    cp_wuv.wait()
    col = iota((HEAD_DIM + ROPE, 384), 0)
    out = iota((HEAD_DIM + ROPE, 384), 1)
    q_arrange = onehot(
        ((out < 192) & (col == out)) | ((out >= 320) & (col == out - 320 + HEAD_DIM))
    )

    def by_head(g):
        rows_g = iota((256, ROWS), 0)
        want_row = (rows_g & (Q_DEV - 1)) * HEADS_DEV + g * 4 + (rows_g >> 6)
        return onehot(iota((256, ROWS), 1) == want_row)

    @pl.loop(0, 4)
    def _(g):
        at = pl.ds(pl.multiple_of(g * 256, 256), 256)
        iq_all[y, :, at] = nn(by_head(g), iq_v[...].reshape(ROWS, IDX_DIM)).astype(BF).T

    for i in range(HEADS_DEV // 2):
        pair = [iw_ref[2 * i + k : 2 * i + k + 1, :] for k in range(2)]
        iw_all[y, i : i + 1, :] = jnp.concatenate(pair, axis=1)

    def iq_copy(d):
        return pltpu.make_async_remote_copy(
            src_ref=iq_all.at[y],
            dst_ref=iq_all.at[y],
            send_sem=iq_send.at[d - 1],
            recv_sem=iq_recv.at[d - 1],
            device_id=head_peer(d),
            device_id_type=MESH,
        )

    def iw_copy(d):
        return pltpu.make_async_remote_copy(
            src_ref=iw_all.at[y],
            dst_ref=iw_all.at[y],
            send_sem=iw_send.at[d - 1],
            recv_sem=iw_recv.at[d - 1],
            device_id=head_peer(d),
            device_id_type=MESH,
        )

    for d in range(1, HEAD_DEVS):
        iq_copy(d).start()
        iw_copy(d).start()

    @pl.loop(0, 4)
    def _(g):
        at = pl.ds(pl.multiple_of(g * 256, 256), 256)
        mine = nn(by_head(g), query_v[...].reshape(ROWS, HEAD_DIM + ROPE)).astype(BF)
        parts = nn(mine, q_arrange).astype(BF)
        lat = [nn(parts[k * 64 : k * 64 + 64, :HEAD_DIM], wuk_v[g * 4 + k]) for k in range(4)]
        qlat[:, at] = jnp.concatenate(lat, axis=0).astype(BF).T
        qra[:, at] = parts[:, 128:256].T
        qrb[:, at] = parts[:, 256:384].T

    @pl.loop(0, HEADS_DEV)
    def _(h):
        wuv_t[h] = wuv_v[h].T

    asked_rel = want[...].reshape(CTX_DEVS, 128).astype(BF)
    rank = nn(asked_rel, before)
    row_count = nn(asked_rel, jnp.ones((128, 128), BF))
    earlier = onehot(iota((CTX_DEVS, CTX_DEVS), 1) < iota((CTX_DEVS, CTX_DEVS), 0))
    ahead = nn(earlier, row_count.astype(BF))
    place = asked_rel.astype(F32) * (ahead + rank + 1.0)
    place_row = jnp.sum(nn(place.astype(BF), slot) * holder, axis=0, keepdims=True)
    place_log = nt(log_lo, (log_hi.astype(F32) * place_row).astype(BF))
    looked = nn(place_log.astype(BF), sel_hi) * sel_lo.astype(F32)
    pos_sel = jnp.sum(looked, axis=0, keepdims=True)
    member = jnp.zeros((POOL, 128), F32)
    pool_id = iota((POOL, 128), 0).astype(F32) + 1.0
    for i in range(NSEL // 2):
        part = pos_sel[:, i * 128 : (i + 1) * 128]
        posn[i : i + 1, :] = part
        member = member + jnp.where(jnp.abs(pool_id - part) < 0.5, 1.0, 0.0)
    member = member + pltpu.roll(member, 64, 1)
    allowed = jnp.broadcast_to(member[:, None, :], (POOL, PART, 128)).reshape(PART_KEYS, 128)
    bias[...] = jnp.where(allowed > 0.5, 0.0, NEG)

    count_lane = nt(jnp.ones((8, 128), BF), asked_rel)
    ahead_lane = nn(
        count_lane.astype(BF), onehot(iota((CTX_DEVS, CTX_DEVS), 0) < iota((CTX_DEVS, CTX_DEVS), 1))
    )
    count_lane = count_lane[0:1, :]
    ahead_lane = ahead_lane[0:1, :]
    lane_of = onehot(iota((CTX_DEVS, PART_KEYS), 0) == (iota((CTX_DEVS, PART_KEYS), 1) >> 4))
    pool_row = iota((POOL, CTX_DEVS), 0).astype(F32)
    for k, pack in ((0, pack0), (1, pack1)):
        hit = (jnp.abs(ahead_lane + float(k) - pool_row) < 0.5) & (count_lane > k + 0.5)
        pack[...] = nn(onehot(hit), lane_of)

    top[...] = jnp.full(top.shape, NEG, F32)
    total[...] = jnp.zeros(total.shape, F32)
    acc[...] = jnp.zeros(acc.shape, F32)

    def direct(way, part, what):
        ref, size = ((kv, PIECE), (rp, PIECE // 2))[what]
        at = ref.at[y, pl.ds(part * size, size)]
        return pltpu.make_async_remote_copy(
            src_ref=at,
            dst_ref=at,
            send_sem=ag_send.at[way, part, what],
            recv_sem=ag_recv.at[way, part, what],
            device_id=head_peer((1, 3)[way]),
            device_id_type=MESH,
        )

    def forward(way, part, what):
        ref, size = ((kv, PIECE), (rp, PIECE // 2))[what]
        origin = lax.rem(y + (3, 1)[way], HEAD_DEVS)
        at = ref.at[origin, pl.ds(part * size + way * (size // 2), size // 2)]
        return pltpu.make_async_remote_copy(
            src_ref=at,
            dst_ref=at,
            send_sem=fw_send.at[way, part, what],
            recv_sem=fw_recv.at[way, part, what],
            device_id=head_peer((1, 3)[way]),
            device_id_type=MESH,
        )

    dup = onehot((iota((128, 128), 0) & 63) == (iota((128, 128), 1) & 63))

    def compact(part):
        blocks = 32 + 8 * (part + 1)
        depth = blocks * PART
        at = slice(part * 16, part * 16 + 16)
        same_row = iota((1, PART, depth), 1) == (iota((1, PART, depth), 2) & (PART - 1))
        move = []
        for pack in (pack0, pack1):
            wide = jnp.where(same_row, pack[at, :depth][:, None, :], 0.0)
            move.append(wide.reshape(PIECE, depth).astype(BF))
        flat = recv[:blocks].reshape(depth, PAIR)
        kv[y, part * PIECE : part * PIECE + PIECE, :] = (
            nn(move[0], flat[:, 0:512]) + nn(move[1], flat[:, 512:1024])
        ).astype(BF)
        ropes = flat[:, 1280:1408]
        ropes0 = jnp.where(low, ropes, jnp.zeros_like(ropes))
        ropes1 = jnp.where(low, jnp.zeros_like(ropes), ropes)
        twice = nn((nn(move[0], ropes0) + nn(move[1], ropes1)).astype(BF), dup).astype(BF)
        rp[y, part * (PIECE // 2) : (part + 1) * (PIECE // 2), :] = jnp.where(
            low, twice[: PIECE // 2], twice[PIECE // 2 :]
        )
        for way in range(2):
            for what in range(2):
                direct(way, part, what).start()
        return (nn(move[0], flat[:, 1024:1152]) + nn(move[1], flat[:, 1152:1280])).astype(BF)

    def pass_on(part):
        for way in range(2):
            for what in range(2):
                direct(way, part, what).wait_recv()
                forward(way, part, what).start()

    def index(part, keys):
        def heads(j, sums):
            raw = jnp.maximum(nn(keys, iq_all[j]), 0.0)
            for i in range(8):
                sums = sums + raw[:, i * 128 : i * 128 + 128] * iw_all[j, i : i + 1, :]
            return sums

        sums = lax.fori_loop(0, HEAD_DEVS, heads, jnp.zeros((PIECE, 128), F32))
        wsum[part * 16 : part * 16 + 16] = (sums + pltpu.roll(sums, 64, 1)).reshape(16, PART, 128)

    factor = (HEAD_DIM + ROPE) ** -0.5 * 1.4426950408889634

    def attend(*pieces):
        keys, scores, masks = [], [], []
        for ahead_y, part in pieces:
            origin = lax.rem(y + ahead_y, HEAD_DEVS)
            keys.append(kv[origin, part * PIECE : part * PIECE + PIECE, :])
            ropes = rp[origin, part * (PIECE // 2) : (part + 1) * (PIECE // 2), :]
            scores += [nn(ropes, qra[...]), nn(ropes, qrb[...])]
            masks.append(bias[part * PIECE : part * PIECE + PIECE, :])
        keys = jnp.concatenate(keys, axis=0)
        mask = jnp.concatenate(masks, axis=0)
        scores = nn(keys, qlat[...]) + jnp.concatenate(scores, axis=0)
        scores = scores + jnp.concatenate([mask] * (ROWS // 128), axis=1)
        old = top[...]
        new = jnp.maximum(old, jnp.max(scores, axis=0, keepdims=True))
        expo = jnp.exp2((scores - new) * factor)
        keep = jnp.exp2((old - new) * factor)
        total[...] = total[...] * keep + jnp.sum(expo, axis=0, keepdims=True)
        acc[...] = acc[...] * keep + nn(keys.T, expo.astype(BF))
        top[...] = new

    def arrived(first, last):
        @pl.loop(first, last)
        def _(s):
            block_copy(s).wait_recv()

    arrived(1, 40)
    keys = compact(0)
    for d in range(1, HEAD_DEVS):
        iq_copy(d).wait_recv()
        iw_copy(d).wait_recv()
    index(0, keys)
    attend((0, 0))

    arrived(40, 48)
    keys = compact(1)
    pass_on(0)
    index(1, keys)
    attend((0, 1), (3, 0), (1, 0))

    arrived(48, 56)
    keys = compact(2)
    pass_on(1)
    index(2, keys)
    for way in range(2):
        for what in range(2):
            forward(way, 0, what).wait_recv()
    attend((0, 2), (2, 0))
    attend((3, 1), (1, 1))

    arrived(56, 64)
    keys = compact(3)
    pass_on(2)
    index(3, keys)

    @pl.loop(0, NSEL // 2)
    def _(i):
        at = posn[pl.ds(i, 1), :] - 1.0
        ids = iota((POOL, PART, 128), 0).astype(F32)
        chosen = jnp.where(jnp.abs(ids - at[None]) < 0.5, wsum[...], 0.0)
        picked[i] = jnp.sum(chosen, axis=0)

    def picked_copy(d):
        to = lax.rem(y + d, HEAD_DEVS)
        return pltpu.make_async_remote_copy(
            src_ref=picked.at[pl.ds(to * 4, 4)],
            dst_ref=picked_in.at[y],
            send_sem=pk_send.at[d - 1],
            recv_sem=pk_recv.at[d - 1],
            device_id=head_peer(d),
            device_id_type=MESH,
        )

    for d in range(1, HEAD_DEVS):
        picked_copy(d).start()
    picked_in[y] = picked[pl.ds(y * 4, 4)]

    for way in range(2):
        for what in range(2):
            forward(way, 1, what).wait_recv()
    attend((0, 3), (2, 1))
    attend((3, 2), (1, 2))
    pass_on(3)
    for way in range(2):
        for what in range(2):
            forward(way, 2, what).wait_recv()
    attend((2, 2), (3, 3), (1, 3))
    for way in range(2):
        for what in range(2):
            forward(way, 3, what).wait_recv()
    attend((2, 3))

    for m in range(HEADS_DEV // 2):
        at = slice(m * 128, m * 128 + 128)
        context = (acc[:, at] / total[:, at]).astype(BF)
        both = nn(wuv_t[2 * m : 2 * m + 2].reshape(256, LATENT), context)
        joined = jnp.where(low, both[:128], both[128:]).T
        attn_ref[:, 2 * m * HEAD_DIM : (2 * m + 1) * HEAD_DIM] = joined[:Q_DEV].astype(BF)
        attn_ref[:, (2 * m + 1) * HEAD_DIM : (2 * m + 2) * HEAD_DIM] = joined[Q_DEV:].astype(BF)

    for d in range(1, HEAD_DEVS):
        picked_copy(d).wait_recv()
    for i in range(4):
        even = jnp.concatenate([picked_in[j, i] for j in range(HEAD_DEVS)], axis=0)
        both = jnp.concatenate([even, pltpu.roll(even, 64, 1)], axis=0)
        idx_ref[:, i * 128 : (i + 1) * 128] = both.T[:Q_DEV, :]

    @pl.loop(1, CTX_DEVS)
    def _(s):
        request(s).wait_send()
        block_copy(s).wait_send()

    for d in range(1, HEAD_DEVS):
        iq_copy(d).wait_send()
        iw_copy(d).wait_send()
        picked_copy(d).wait_send()
    for way in range(2):
        for what in range(2):
            for part in range(PARTS):
                direct(way, part, what).wait_send()
                forward(way, part, what).wait_send()


def shards(
    query, w_uk, w_uv, index_query, index_weight, cache_rows, key_scale, selected, block_home
):
    vmem = pl.BlockSpec(memory_space=pltpu.VMEM)
    hbm = pl.BlockSpec(memory_space=pl.ANY)
    dma = pltpu.SemaphoreType.DMA
    width = cache_rows.shape[1]
    attn, idx = pl.pallas_call(
        kernel,
        out_shape=(
            jax.ShapeDtypeStruct((Q_DEV, HEADS_DEV * HEAD_DIM), BF),
            jax.ShapeDtypeStruct((Q_DEV, NSEL * BLOCK // HEAD_DEVS), F32),
        ),
        in_specs=[vmem] * 4 + [hbm] * 5,
        out_specs=(vmem, vmem),
        scratch_shapes=[
            pltpu.VMEM((width, BLK_DEV * BLOCK), BF),
            pltpu.VMEM(query.shape, BF),
            pltpu.VMEM(index_query.shape, BF),
            pltpu.VMEM(w_uk.shape, BF),
            pltpu.VMEM(w_uv.shape, BF),
            pltpu.VMEM((HEADS_DEV, HEAD_DIM, LATENT), BF),
            pltpu.VMEM((CTX_DEVS, 1, 128), F32),
            pltpu.VMEM((CTX_DEVS, 1, 128), F32),
            pltpu.VMEM((BLK_DEV * PART, LATENT + 384), BF),
            pltpu.VMEM((2, CTX_DEVS, 512), F32),
            pltpu.VMEM((CTX_DEVS, PART, PAIR), BF),
            pltpu.VMEM((CTX_DEVS, PART, PAIR), BF),
            pltpu.VMEM((NSEL // 2, 128), F32),
            pltpu.VMEM((PART_KEYS, 128), F32),
            pltpu.VMEM((POOL, PART_KEYS), F32),
            pltpu.VMEM((POOL, PART_KEYS), F32),
            pltpu.VMEM((HEAD_DEVS, PART_KEYS, LATENT), BF),
            pltpu.VMEM((HEAD_DEVS, PART_KEYS // 2, 128), BF),
            pltpu.VMEM((HEAD_DEVS, IDX_DIM, ROWS), BF),
            pltpu.VMEM((HEAD_DEVS, 8, 128), F32),
            pltpu.VMEM((LATENT, ROWS), BF),
            pltpu.VMEM((128, ROWS), BF),
            pltpu.VMEM((128, ROWS), BF),
            pltpu.VMEM((POOL, PART, 128), F32),
            pltpu.VMEM((NSEL // 2, PART, 128), F32),
            pltpu.VMEM((HEAD_DEVS, NSEL // 8, PART, 128), F32),
            pltpu.VMEM((1, ROWS), F32),
            pltpu.VMEM((1, ROWS), F32),
            pltpu.VMEM((LATENT, ROWS), F32),
            dma((5,)),
            dma((CTX_DEVS,)),
            dma((CTX_DEVS,)),
            dma((CTX_DEVS,)),
            dma((CTX_DEVS,)),
            dma((3,)),
            dma((3,)),
            dma((3,)),
            dma((3,)),
            dma((3,)),
            dma((3,)),
            dma((2, PARTS, 2)),
            dma((2, PARTS, 2)),
            dma((2, PARTS, 2)),
            dma((2, PARTS, 2)),
        ],
        compiler_params=pltpu.CompilerParams(
            collective_id=0, has_side_effects=True, vmem_limit_bytes=58 * 1024 * 1024
        ),
    )(
        selected.T,
        block_home.reshape(1, NBLK),
        key_scale.reshape(1, BLK_DEV * BLOCK),
        index_weight.T,
        query,
        index_query,
        cache_rows.T,
        w_uk,
        w_uv,
    )
    return (attn.reshape(Q_DEV, HEADS_DEV, HEAD_DIM), idx)


def solution(mesh):
    return jax.shard_map(
        shards,
        mesh=mesh,
        in_specs=(
            P("ctx", "head", None),
            P("head", None, None),
            P("head", None, None),
            P("ctx", "head", None),
            P("ctx", "head"),
            P("ctx", None),
            P("ctx"),
            P("ctx", None),
            P(),
        ),
        out_specs=(P("ctx", "head", None), P("ctx", "head")),
        check_vma=False,
    )
```

```python
import jax
import jax.numpy as jnp
from jax import lax
from jax.experimental import pallas as pl
from jax.experimental.pallas import tpu as pltpu
from jax.sharding import PartitionSpec as P

LATENT = 512
ROPE = 64
HEAD_DIM = 128
IDX_DIM = 128
BLOCK = 64
NSEL = 32
POOL = 64
BLK_DEV = 32
NBLK = 2048
Q_DEV = 64
HEADS_DEV = 16
CTX_DEVS = 64
HEAD_DEVS = 4
PART = BLOCK // HEAD_DEVS
ROWS = HEADS_DEV * Q_DEV
PART_KEYS = POOL * PART
PARTS = 4
PIECE = PART_KEYS // PARTS
PAIR = 2 * LATENT + 2 * IDX_DIM + 2 * ROPE
NEG = -1e30
MESH = pl.DeviceIdType.MESH
BF = jnp.bfloat16
F32 = jnp.float32


def nn(a, b):
    return jnp.dot(a, b, preferred_element_type=F32)


def nt(a, b):
    return lax.dot_general(a, b, (((1,), (1,)), ((), ())), preferred_element_type=F32)


def iota(shape, dim):
    return lax.broadcasted_iota(jnp.int32, shape, dim)


def onehot(cond):
    return jnp.where(cond, 1.0, 0.0).astype(BF)


def kernel(
    sel_ref,
    home_ref,
    scale_ref,
    iw_ref,
    query_hbm,
    iq_hbm,
    cache_hbm,
    wuk_hbm,
    wuv_hbm,
    attn_ref,
    idx_ref,
    cache_v,
    query_v,
    iq_v,
    wuk_v,
    wuv_v,
    wuv_t,
    want,
    want_in,
    weights,
    expand,
    served,
    recv,
    posn,
    bias,
    pack0,
    pack1,
    kv,
    rp,
    iq_all,
    iw_all,
    qlat,
    qra,
    qrb,
    wsum,
    picked,
    picked_in,
    top,
    total,
    acc,
    local_sem,
    req_send,
    req_recv,
    blk_send,
    blk_recv,
    iq_send,
    iq_recv,
    iw_send,
    iw_recv,
    pk_send,
    pk_recv,
    ag_send,
    ag_recv,
    fw_send,
    fw_recv,
):
    me = lax.axis_index("ctx")
    y = lax.axis_index("head")

    def ctx_peer(c):
        return (lax.rem(c + 2 * CTX_DEVS, CTX_DEVS), y)

    def head_peer(d):
        return (me, lax.rem(y + d, HEAD_DEVS))

    barrier = pltpu.get_barrier_semaphore()

    @pl.loop(1, CTX_DEVS)
    def _(s):
        pl.semaphore_signal(barrier, inc=1, device_id=ctx_peer(me + s), device_id_type=MESH)

    for d in range(1, HEAD_DEVS):
        pl.semaphore_signal(barrier, inc=1, device_id=head_peer(d), device_id_type=MESH)

    cp_cache = pltpu.make_async_copy(cache_hbm, cache_v, local_sem.at[0])
    cp_query = pltpu.make_async_copy(query_hbm, query_v, local_sem.at[1])
    cp_iq = pltpu.make_async_copy(iq_hbm, iq_v, local_sem.at[2])
    cp_wuk = pltpu.make_async_copy(wuk_hbm, wuk_v, local_sem.at[3])
    cp_wuv = pltpu.make_async_copy(wuv_hbm, wuv_v, local_sem.at[4])
    cp_cache.start()

    sel = jnp.concatenate([sel_ref[i : i + 1, :] for i in range(NSEL)], axis=1)
    home = home_ref[...]
    sel_hi = onehot(iota((32, NBLK), 0) == (sel >> 6))
    sel_lo = onehot(iota((64, NBLK), 0) == (sel & 63))
    lane = iota((1, NBLK), 1)
    log_hi = onehot(iota((32, NBLK), 0) == (lane >> 6))
    log_lo = onehot(iota((64, NBLK), 0) == (lane & 63))
    counts = nt(sel_hi, sel_lo)
    wanted = onehot(counts > 0.5)
    wanted_row = jnp.sum(nn(wanted, log_lo) * log_hi.astype(F32), axis=0, keepdims=True)
    rel = (me - (home >> 5)) & (CTX_DEVS - 1)
    holder = jnp.where(iota((CTX_DEVS, NBLK), 0) == rel, 1.0, 0.0)
    slot = onehot(iota((128, NBLK), 0) == (home & (BLK_DEV - 1)))
    want_rel = nt((holder * wanted_row).astype(BF), slot)
    want[...] = want_rel.reshape(CTX_DEVS, 1, 128)
    want_in[0] = want[0]

    pl.semaphore_wait(barrier, CTX_DEVS - 1 + HEAD_DEVS - 1)

    def request(s):
        return pltpu.make_async_remote_copy(
            src_ref=want.at[s],
            dst_ref=want_in.at[s],
            send_sem=req_send.at[s],
            recv_sem=req_recv.at[s],
            device_id=ctx_peer(me - s),
            device_id_type=MESH,
        )

    @pl.loop(1, CTX_DEVS)
    def _(s):
        request(s).start()

    cp_cache.wait()
    for cp in (cp_query, cp_iq, cp_wuk, cp_wuv):
        cp.start()
    row = iota((BLK_DEV * PART, NBLK), 0)
    mine = onehot(iota((BLK_DEV * PART, NBLK), 1) == (row >> 4) * BLOCK + y * PART + (row & 15))
    scaled = (cache_v[LATENT + ROPE :, :].astype(F32) * scale_ref[...]).astype(BF)
    rope = cache_v[LATENT : LATENT + ROPE, :]
    weights[:, :LATENT] = nt(mine, cache_v[:LATENT, :]).astype(BF)
    weights[:, LATENT : LATENT + IDX_DIM] = nt(mine, scaled).astype(BF)
    ropes = nt(mine, jnp.concatenate([rope, rope], axis=0)).astype(BF)
    low = iota((1, 128), 1) < ROPE
    weights[:, LATENT + 128 : LATENT + 256] = jnp.where(low, ropes, jnp.zeros_like(ropes))
    weights[:, LATENT + 256 :] = jnp.where(low, jnp.zeros_like(ropes), ropes)

    @pl.loop(1, CTX_DEVS)
    def _(s):
        request(s).wait_recv()

    asked = want_in[...].reshape(CTX_DEVS, 128)
    before = onehot(iota((128, 128), 0) < iota((128, 128), 1))
    order = nn(asked.astype(BF), before)
    spread = onehot(iota((128, 512), 0) == (iota((128, 512), 1) >> 4))
    for k in range(2):
        first = jnp.where(jnp.abs(order - float(k)) < 0.5, asked, 0.0)
        expand[k] = nn(first.astype(BF), spread)

    def block_copy(s):
        return pltpu.make_async_remote_copy(
            src_ref=served.at[s],
            dst_ref=recv.at[s],
            send_sem=blk_send.at[s],
            recv_sem=blk_recv.at[s],
            device_id=ctx_peer(me + s),
            device_id_type=MESH,
        )

    group = 16

    @pl.loop(0, CTX_DEVS // group)
    def _(i):
        at = pl.ds(pl.multiple_of(i * group, group), group)
        same_row = iota((1, PART, 512), 1) == (iota((1, PART, 512), 2) & (PART - 1))
        gather = []
        for k in range(2):
            wide = jnp.where(same_row, expand[k, at, :][:, None, :], 0.0)
            gather.append(wide.reshape(group * PART, 512).astype(BF))
        o0 = nn(gather[0], weights[:, : LATENT + 256]).astype(BF)
        o1 = nn(gather[1], weights[:, : LATENT + IDX_DIM]).astype(BF)
        r1 = nn(gather[1], weights[:, LATENT + 256 :]).astype(BF)
        shape = (group, PART, -1)
        served[at, :, 0:512] = o0[:, :512].reshape(shape)
        served[at, :, 512:1024] = o1[:, :512].reshape(shape)
        served[at, :, 1024:1152] = o0[:, 512:640].reshape(shape)
        served[at, :, 1152:1280] = o1[:, 512:640].reshape(shape)
        served[at, :, 1280:1408] = (o0[:, 640:768] + r1).reshape(shape)

        @pl.loop(jnp.where(i == 0, 1, 0), group)
        def _(j):
            block_copy(i * group + j).start()

    recv[0] = served[0]

    cp_query.wait()
    cp_iq.wait()
    cp_wuk.wait()
    cp_wuv.wait()
    col = iota((HEAD_DIM + ROPE, 384), 0)
    out = iota((HEAD_DIM + ROPE, 384), 1)
    q_arrange = onehot(
        ((out < 192) & (col == out)) | ((out >= 320) & (col == out - 320 + HEAD_DIM))
    )

    def by_head(g):
        rows_g = iota((256, ROWS), 0)
        want_row = (rows_g & (Q_DEV - 1)) * HEADS_DEV + g * 4 + (rows_g >> 6)
        return onehot(iota((256, ROWS), 1) == want_row)

    @pl.loop(0, 4)
    def _(g):
        at = pl.ds(pl.multiple_of(g * 256, 256), 256)
        iq_all[y, :, at] = nn(by_head(g), iq_v[...].reshape(ROWS, IDX_DIM)).astype(BF).T

    for i in range(HEADS_DEV // 2):
        pair = [iw_ref[2 * i + k : 2 * i + k + 1, :] for k in range(2)]
        iw_all[y, i : i + 1, :] = jnp.concatenate(pair, axis=1)

    def iq_copy(d):
        return pltpu.make_async_remote_copy(
            src_ref=iq_all.at[y],
            dst_ref=iq_all.at[y],
            send_sem=iq_send.at[d - 1],
            recv_sem=iq_recv.at[d - 1],
            device_id=head_peer(d),
            device_id_type=MESH,
        )

    def iw_copy(d):
        return pltpu.make_async_remote_copy(
            src_ref=iw_all.at[y],
            dst_ref=iw_all.at[y],
            send_sem=iw_send.at[d - 1],
            recv_sem=iw_recv.at[d - 1],
            device_id=head_peer(d),
            device_id_type=MESH,
        )

    for d in range(1, HEAD_DEVS):
        iq_copy(d).start()
        iw_copy(d).start()

    @pl.loop(0, 4)
    def _(g):
        at = pl.ds(pl.multiple_of(g * 256, 256), 256)
        mine = nn(by_head(g), query_v[...].reshape(ROWS, HEAD_DIM + ROPE)).astype(BF)
        parts = nn(mine, q_arrange).astype(BF)
        lat = [nn(parts[k * 64 : k * 64 + 64, :HEAD_DIM], wuk_v[g * 4 + k]) for k in range(4)]
        qlat[:, at] = jnp.concatenate(lat, axis=0).astype(BF).T
        qra[:, at] = parts[:, 128:256].T
        qrb[:, at] = parts[:, 256:384].T

    @pl.loop(0, HEADS_DEV)
    def _(h):
        wuv_t[h] = wuv_v[h].T

    asked_rel = want[...].reshape(CTX_DEVS, 128).astype(BF)
    rank = nn(asked_rel, before)
    row_count = nn(asked_rel, jnp.ones((128, 128), BF))
    earlier = onehot(iota((CTX_DEVS, CTX_DEVS), 1) < iota((CTX_DEVS, CTX_DEVS), 0))
    ahead = nn(earlier, row_count.astype(BF))
    place = asked_rel.astype(F32) * (ahead + rank + 1.0)
    place_row = jnp.sum(nn(place.astype(BF), slot) * holder, axis=0, keepdims=True)
    place_log = nt(log_lo, (log_hi.astype(F32) * place_row).astype(BF))
    looked = nn(place_log.astype(BF), sel_hi) * sel_lo.astype(F32)
    pos_sel = jnp.sum(looked, axis=0, keepdims=True)
    member = jnp.zeros((POOL, 128), F32)
    pool_id = iota((POOL, 128), 0).astype(F32) + 1.0
    for i in range(NSEL // 2):
        part = pos_sel[:, i * 128 : (i + 1) * 128]
        posn[i : i + 1, :] = part
        member = member + jnp.where(jnp.abs(pool_id - part) < 0.5, 1.0, 0.0)
    member = member + pltpu.roll(member, 64, 1)
    allowed = jnp.broadcast_to(member[:, None, :], (POOL, PART, 128)).reshape(PART_KEYS, 128)
    bias[...] = jnp.where(allowed > 0.5, 0.0, NEG)

    count_lane = nt(jnp.ones((8, 128), BF), asked_rel)
    ahead_lane = nn(
        count_lane.astype(BF), onehot(iota((CTX_DEVS, CTX_DEVS), 0) < iota((CTX_DEVS, CTX_DEVS), 1))
    )
    count_lane = count_lane[0:1, :]
    ahead_lane = ahead_lane[0:1, :]
    lane_of = onehot(iota((CTX_DEVS, PART_KEYS), 0) == (iota((CTX_DEVS, PART_KEYS), 1) >> 4))
    pool_row = iota((POOL, CTX_DEVS), 0).astype(F32)
    for k, pack in ((0, pack0), (1, pack1)):
        hit = (jnp.abs(ahead_lane + float(k) - pool_row) < 0.5) & (count_lane > k + 0.5)
        pack[...] = nn(onehot(hit), lane_of)

    top[...] = jnp.full(top.shape, NEG, F32)
    total[...] = jnp.zeros(total.shape, F32)
    acc[...] = jnp.zeros(acc.shape, F32)

    def direct(way, part, what):
        ref, size = ((kv, PIECE), (rp, PIECE // 2))[what]
        at = ref.at[y, pl.ds(part * size, size)]
        return pltpu.make_async_remote_copy(
            src_ref=at,
            dst_ref=at,
            send_sem=ag_send.at[way, part, what],
            recv_sem=ag_recv.at[way, part, what],
            device_id=head_peer((1, 3)[way]),
            device_id_type=MESH,
        )

    def forward(way, part, what):
        ref, size = ((kv, PIECE), (rp, PIECE // 2))[what]
        origin = lax.rem(y + (3, 1)[way], HEAD_DEVS)
        at = ref.at[origin, pl.ds(part * size + way * (size // 2), size // 2)]
        return pltpu.make_async_remote_copy(
            src_ref=at,
            dst_ref=at,
            send_sem=fw_send.at[way, part, what],
            recv_sem=fw_recv.at[way, part, what],
            device_id=head_peer((1, 3)[way]),
            device_id_type=MESH,
        )

    dup = onehot((iota((128, 128), 0) & 63) == (iota((128, 128), 1) & 63))

    def compact(part):
        blocks = 32 + 8 * (part + 1)
        depth = blocks * PART
        at = slice(part * 16, part * 16 + 16)
        same_row = iota((1, PART, depth), 1) == (iota((1, PART, depth), 2) & (PART - 1))
        move = []
        for pack in (pack0, pack1):
            wide = jnp.where(same_row, pack[at, :depth][:, None, :], 0.0)
            move.append(wide.reshape(PIECE, depth).astype(BF))
        flat = recv[:blocks].reshape(depth, PAIR)
        kv[y, part * PIECE : part * PIECE + PIECE, :] = (
            nn(move[0], flat[:, 0:512]) + nn(move[1], flat[:, 512:1024])
        ).astype(BF)
        ropes = flat[:, 1280:1408]
        ropes0 = jnp.where(low, ropes, jnp.zeros_like(ropes))
        ropes1 = jnp.where(low, jnp.zeros_like(ropes), ropes)
        twice = nn((nn(move[0], ropes0) + nn(move[1], ropes1)).astype(BF), dup).astype(BF)
        rp[y, part * (PIECE // 2) : (part + 1) * (PIECE // 2), :] = jnp.where(
            low, twice[: PIECE // 2], twice[PIECE // 2 :]
        )
        for way in range(2):
            for what in range(2):
                direct(way, part, what).start()
        return (nn(move[0], flat[:, 1024:1152]) + nn(move[1], flat[:, 1152:1280])).astype(BF)

    def pass_on(part):
        for way in range(2):
            for what in range(2):
                direct(way, part, what).wait_recv()
                forward(way, part, what).start()

    def index(part, keys):
        def heads(j, sums):
            raw = jnp.maximum(nn(keys, iq_all[j]), 0.0)
            for i in range(8):
                sums = sums + raw[:, i * 128 : i * 128 + 128] * iw_all[j, i : i + 1, :]
            return sums

        sums = lax.fori_loop(0, HEAD_DEVS, heads, jnp.zeros((PIECE, 128), F32))
        wsum[part * 16 : part * 16 + 16] = (sums + pltpu.roll(sums, 64, 1)).reshape(16, PART, 128)

    factor = (HEAD_DIM + ROPE) ** -0.5 * 1.4426950408889634

    def attend(*pieces):
        keys, scores, masks = [], [], []
        for ahead_y, part in pieces:
            origin = lax.rem(y + ahead_y, HEAD_DEVS)
            keys.append(kv[origin, part * PIECE : part * PIECE + PIECE, :])
            ropes = rp[origin, part * (PIECE // 2) : (part + 1) * (PIECE // 2), :]
            scores += [nn(ropes, qra[...]), nn(ropes, qrb[...])]
            masks.append(bias[part * PIECE : part * PIECE + PIECE, :])
        keys = jnp.concatenate(keys, axis=0)
        mask = jnp.concatenate(masks, axis=0)
        scores = nn(keys, qlat[...]) + jnp.concatenate(scores, axis=0)
        scores = scores + jnp.concatenate([mask] * (ROWS // 128), axis=1)
        old = top[...]
        new = jnp.maximum(old, jnp.max(scores, axis=0, keepdims=True))
        expo = jnp.exp2((scores - new) * factor)
        keep = jnp.exp2((old - new) * factor)
        total[...] = total[...] * keep + jnp.sum(expo, axis=0, keepdims=True)
        acc[...] = acc[...] * keep + nn(keys.T, expo.astype(BF))
        top[...] = new

    def arrived(first, last):
        @pl.loop(first, last)
        def _(s):
            block_copy(s).wait_recv()

    arrived(1, 40)
    keys = compact(0)
    for d in range(1, HEAD_DEVS):
        iq_copy(d).wait_recv()
        iw_copy(d).wait_recv()
    index(0, keys)
    attend((0, 0))

    arrived(40, 48)
    keys = compact(1)
    pass_on(0)
    index(1, keys)
    attend((0, 1), (3, 0), (1, 0))

    arrived(48, 56)
    keys = compact(2)
    pass_on(1)
    index(2, keys)
    for way in range(2):
        for what in range(2):
            forward(way, 0, what).wait_recv()
    attend((0, 2), (2, 0))
    attend((3, 1), (1, 1))

    arrived(56, 64)
    keys = compact(3)
    pass_on(2)
    index(3, keys)

    @pl.loop(0, NSEL // 2)
    def _(i):
        at = posn[pl.ds(i, 1), :] - 1.0
        ids = iota((POOL, PART, 128), 0).astype(F32)
        chosen = jnp.where(jnp.abs(ids - at[None]) < 0.5, wsum[...], 0.0)
        picked[i] = jnp.sum(chosen, axis=0)

    def picked_copy(d):
        to = lax.rem(y + d, HEAD_DEVS)
        return pltpu.make_async_remote_copy(
            src_ref=picked.at[pl.ds(to * 4, 4)],
            dst_ref=picked_in.at[y],
            send_sem=pk_send.at[d - 1],
            recv_sem=pk_recv.at[d - 1],
            device_id=head_peer(d),
            device_id_type=MESH,
        )

    for d in range(1, HEAD_DEVS):
        picked_copy(d).start()
    picked_in[y] = picked[pl.ds(y * 4, 4)]

    for way in range(2):
        for what in range(2):
            forward(way, 1, what).wait_recv()
    attend((0, 3), (2, 1))
    attend((3, 2), (1, 2))
    pass_on(3)
    for way in range(2):
        for what in range(2):
            forward(way, 2, what).wait_recv()
    attend((2, 2), (3, 3), (1, 3))
    for d in range(1, HEAD_DEVS):
        picked_copy(d).wait_recv()
    for i in range(4):
        even = jnp.concatenate([picked_in[j, i] for j in range(HEAD_DEVS)], axis=0)
        both = jnp.concatenate([even, pltpu.roll(even, 64, 1)], axis=0)
        idx_ref[:, i * 128 : (i + 1) * 128] = both.T[:Q_DEV, :]

    for way in range(2):
        for what in range(2):
            forward(way, 3, what).wait_recv()
    attend((2, 3))

    for m in range(HEADS_DEV // 2):
        at = slice(m * 128, m * 128 + 128)
        context = (acc[:, at] / total[:, at]).astype(BF)
        both = nn(wuv_t[2 * m : 2 * m + 2].reshape(256, LATENT), context)
        joined = jnp.where(low, both[:128], both[128:]).T
        attn_ref[:, 2 * m * HEAD_DIM : (2 * m + 1) * HEAD_DIM] = joined[:Q_DEV].astype(BF)
        attn_ref[:, (2 * m + 1) * HEAD_DIM : (2 * m + 2) * HEAD_DIM] = joined[Q_DEV:].astype(BF)

    @pl.loop(1, CTX_DEVS)
    def _(s):
        request(s).wait_send()
        block_copy(s).wait_send()

    for d in range(1, HEAD_DEVS):
        iq_copy(d).wait_send()
        iw_copy(d).wait_send()
        picked_copy(d).wait_send()
    for way in range(2):
        for what in range(2):
            for part in range(PARTS):
                direct(way, part, what).wait_send()
                forward(way, part, what).wait_send()


def shards(
    query, w_uk, w_uv, index_query, index_weight, cache_rows, key_scale, selected, block_home
):
    vmem = pl.BlockSpec(memory_space=pltpu.VMEM)
    hbm = pl.BlockSpec(memory_space=pl.ANY)
    dma = pltpu.SemaphoreType.DMA
    width = cache_rows.shape[1]
    attn, idx = pl.pallas_call(
        kernel,
        out_shape=(
            jax.ShapeDtypeStruct((Q_DEV, HEADS_DEV * HEAD_DIM), BF),
            jax.ShapeDtypeStruct((Q_DEV, NSEL * BLOCK // HEAD_DEVS), F32),
        ),
        in_specs=[vmem] * 4 + [hbm] * 5,
        out_specs=(vmem, vmem),
        scratch_shapes=[
            pltpu.VMEM((width, BLK_DEV * BLOCK), BF),
            pltpu.VMEM(query.shape, BF),
            pltpu.VMEM(index_query.shape, BF),
            pltpu.VMEM(w_uk.shape, BF),
            pltpu.VMEM(w_uv.shape, BF),
            pltpu.VMEM((HEADS_DEV, HEAD_DIM, LATENT), BF),
            pltpu.VMEM((CTX_DEVS, 1, 128), F32),
            pltpu.VMEM((CTX_DEVS, 1, 128), F32),
            pltpu.VMEM((BLK_DEV * PART, LATENT + 384), BF),
            pltpu.VMEM((2, CTX_DEVS, 512), F32),
            pltpu.VMEM((CTX_DEVS, PART, PAIR), BF),
            pltpu.VMEM((CTX_DEVS, PART, PAIR), BF),
            pltpu.VMEM((NSEL // 2, 128), F32),
            pltpu.VMEM((PART_KEYS, 128), F32),
            pltpu.VMEM((POOL, PART_KEYS), F32),
            pltpu.VMEM((POOL, PART_KEYS), F32),
            pltpu.VMEM((HEAD_DEVS, PART_KEYS, LATENT), BF),
            pltpu.VMEM((HEAD_DEVS, PART_KEYS // 2, 128), BF),
            pltpu.VMEM((HEAD_DEVS, IDX_DIM, ROWS), BF),
            pltpu.VMEM((HEAD_DEVS, 8, 128), F32),
            pltpu.VMEM((LATENT, ROWS), BF),
            pltpu.VMEM((128, ROWS), BF),
            pltpu.VMEM((128, ROWS), BF),
            pltpu.VMEM((POOL, PART, 128), F32),
            pltpu.VMEM((NSEL // 2, PART, 128), F32),
            pltpu.VMEM((HEAD_DEVS, NSEL // 8, PART, 128), F32),
            pltpu.VMEM((1, ROWS), F32),
            pltpu.VMEM((1, ROWS), F32),
            pltpu.VMEM((LATENT, ROWS), F32),
            dma((5,)),
            dma((CTX_DEVS,)),
            dma((CTX_DEVS,)),
            dma((CTX_DEVS,)),
            dma((CTX_DEVS,)),
            dma((3,)),
            dma((3,)),
            dma((3,)),
            dma((3,)),
            dma((3,)),
            dma((3,)),
            dma((2, PARTS, 2)),
            dma((2, PARTS, 2)),
            dma((2, PARTS, 2)),
            dma((2, PARTS, 2)),
        ],
        compiler_params=pltpu.CompilerParams(
            collective_id=0, has_side_effects=True, vmem_limit_bytes=58 * 1024 * 1024
        ),
    )(
        selected.T,
        block_home.reshape(1, NBLK),
        key_scale.reshape(1, BLK_DEV * BLOCK),
        index_weight.T,
        query,
        index_query,
        cache_rows.T,
        w_uk,
        w_uv,
    )
    return (attn.reshape(Q_DEV, HEADS_DEV, HEAD_DIM), idx)


def solution(mesh):
    return jax.shard_map(
        shards,
        mesh=mesh,
        in_specs=(
            P("ctx", "head", None),
            P("head", None, None),
            P("head", None, None),
            P("ctx", "head", None),
            P("ctx", "head"),
            P("ctx", None),
            P("ctx"),
            P("ctx", None),
            P(),
        ),
        out_specs=(P("ctx", "head", None), P("ctx", "head")),
        check_vma=False,
    )
```
